256 devices in a mesh: seq: 16 (over y_hi, z), tp: 2 (over y_lo), head: 8 (over x, core).
Axes of the slice: x: 4, y: 4 (y_hi: 2, y_lo: 2; y = y_hi * 2 + y_lo), z: 8, core: 2. Of those that a mesh axis runs over, the one named last changes fastest.
Arguments:
- tokens: bfloat16 [81920, 8192], P(('seq', 'head')), may hold values from -60 to 60
- kv_weight: bfloat16 [8192, 2048], P('seq', 'tp'), may hold values from -0.0625 to 0.0625
- lengths: int32 [2], replicated, may hold values from 20480 to 40960, as said below
- page_table: int32 [320], P(('seq', 'tp')), may hold values from 0 to 9, as said below
- queries: bfloat16 [2, 64, 8192], P(None, None, 'head'), may hold values from -180 to 180
- new_keys: bfloat16 [2, 64, 1024], P(None, None, 'head'), may hold values from -6 to 6
- new_values: bfloat16 [2, 64, 1024], P(None, None, 'head'), may hold values from -6 to 6
- positions: int32 [2, 64], replicated, may hold values from 1 to 40960
Outputs:
- kv_cache: bfloat16 [2, 320, 256, 1024], P(None, ('seq', 'tp'), None, 'head')
- scales: float32 [2, 1024], replicated
- attended: bfloat16 [2, 64, 8192], P(None, None, 'head')
The draws below stay inside these ranges and needn't reach their ends.
Inputs may be any that keep to these rules, and one draw needn't show every extreme that they name: `lengths`: one of the two prompts has all 40960 tokens valid, the other at least half of them. `page_table`: each aligned group of 10 entries is a permutation of 0 to 9.
All inputs are finite; a program needn't handle non-finite values.
Results may differ from the reference program's by a relative error of at most 0.0041.
The reference program's roundings to bfloat16 on the way (of `quant`, `scaled` and `weight`) count: a program that leaves them out, or rounds other values in their place, can miss the bound.
Values may be sent and summed in bfloat16 or wider, within the bound.
No kernel may reach another device: no remote copies, remote signals or barrier semaphores. Data moves between devices by JAX's collectives and lax.ppermute only.
A program may use at most 128 MiB of HBM per device.

```python
import math
import jax
import jax.numpy as jnp
from jax import lax

D = 8192
KVH = 8
HD = 128
QH = 64
PAGE = 256
STEPS = 2
ROWS = 64
TOKENS = 81920
PROMPT = 40960
PAGES = 320
PAGES_DEV = 10
GROUP = 8


def shared_lengths(key):
    first_key, second_key = jax.random.split(key)
    other = jax.random.randint(first_key, (), PROMPT // 2, PROMPT + 1)
    which = jax.random.randint(second_key, (), 0, 2)
    return jnp.where(jnp.arange(2) == which, PROMPT, other).astype(jnp.int32)


def draw_lengths(key, part):
    return shared_lengths(key)


def draw_positions(key, part):
    lens = shared_lengths(key)
    key = jax.random.fold_in(key, 5)
    raw_key, shift_key = jax.random.split(key)
    row_prompt = jnp.arange(ROWS, dtype=jnp.int32) // (ROWS // 2)
    limit = lens[row_prompt]
    raw = jax.random.randint(raw_key, (STEPS, ROWS), 0, 2 ** 30)
    shift = jax.random.randint(shift_key, (STEPS, ROWS), 0, 16)
    reach = jnp.maximum(jnp.right_shift(limit[None, :], shift), 1)
    picked = 1 + raw % reach
    picked = picked.at[0, 0].set(lens[0]).at[0, ROWS // 2].set(lens[1])
    return picked.astype(jnp.int32)


def draw_page_table(key, part):
    key = jax.random.fold_in(key, 7)
    group_keys = jax.random.split(key, PAGES // PAGES_DEV)
    orders = jax.vmap(lambda single: jax.random.permutation(single, PAGES_DEV))(group_keys)
    return orders.reshape(PAGES).astype(jnp.int32)


def draw_queries(key, part):
    key = jax.random.fold_in(key, 3)
    value_key = jax.random.fold_in(key, 0)
    values = jnp.clip(jax.random.normal(value_key, (STEPS, ROWS, QH * HD), jnp.float32), -6.0, 6.0)
    return values.astype(jnp.bfloat16)


def draw_tokens(key, part):
    key = jax.random.fold_in(key, 11)
    value_key, scale_key = jax.random.split(key, 2)
    place = (jnp.arange(TOKENS, dtype=jnp.int32) % PROMPT).astype(jnp.float32)
    rise = jnp.exp(math.log(3.0) * place / PROMPT)
    values = jnp.clip(jax.random.normal(value_key, (TOKENS, D), jnp.float32), -6.0, 6.0)
    rough = jnp.exp(jax.random.uniform(scale_key, (TOKENS,), jnp.float32, 0.0, math.log(3.0)))
    return (values * (rise * rough)[:, None]).astype(jnp.bfloat16)


def steps_of(own_key, shape, shards, least, largest):
    def one(axis_at, blocks):
        heights = jax.random.uniform(jax.random.fold_in(jax.random.fold_in(own_key, 6), axis_at), (blocks,), jnp.float32, least / len(shards), largest / len(shards))
        return jnp.repeat(jnp.exp(heights), shape[axis_at] // blocks).reshape((-1,) + (1,) * (len(shape) - axis_at - 1))

    level = one(*shards[0])
    for cut in shards[1:]:
        level = level * one(*cut)
    return level


def centred(stream_key, shape, deviation, most, cuts=(), kind=jnp.bfloat16):
    array = deviation * jax.random.normal(stream_key, shape, jnp.float32)
    if cuts:
        array = array * steps_of(stream_key, shape, cuts, -0.22, 0.18)
    return jnp.clip(array, -most, most).astype(kind)


def setup_inputs(seed: int = 0) -> dict:
    seeds = jax.random.split(jax.random.key(seed), 9)
    return {
        "tokens": draw_tokens(jax.random.fold_in(seeds[8], 71), 0),
        "kv_weight": centred(seeds[1], (D, 2 * KVH * HD), D ** -0.5, 0.0625, ((0, 16), (1, 2))),
        "lengths": draw_lengths(jax.random.fold_in(seeds[8], 71), 0),
        "page_table": draw_page_table(jax.random.fold_in(seeds[8], 71), 0),
        "queries": draw_queries(jax.random.fold_in(seeds[8], 71), 0),
        "new_keys": centred(seeds[5], (STEPS, ROWS, KVH * HD), 1.0, 6.0, ((2, 8),)),
        "new_values": centred(seeds[6], (STEPS, ROWS, KVH * HD), 1.0, 6.0, ((2, 8),)),
        "positions": draw_positions(jax.random.fold_in(seeds[8], 71), 0),
    }


eps = 1e-05
clip_level = 2.5
masked_fill = -1e+30

def reference(tokens, kv_weight, lengths, page_table, queries, new_keys, new_values, positions):
    width = KVH * HD
    proj = jnp.dot(tokens, kv_weight, preferred_element_type=jnp.float32)
    token_ids = jnp.arange(TOKENS, dtype=jnp.int32)
    prompt_of = token_ids // PROMPT
    place = token_ids % PROMPT
    limit = jnp.where(prompt_of == 0, lengths[0], lengths[1])
    valid = place < limit
    squares = lax.optimization_barrier(jnp.sum(jnp.where(valid[:, None], proj * proj, 0.0), axis=0)).reshape(2, width)
    count = (lengths[0] + lengths[1]).astype(jnp.float32)
    scales = jnp.sqrt(squares / count + eps)
    quant = jnp.clip(proj.reshape(TOKENS, 2, width) / scales[None], -clip_level, clip_level).astype(jnp.bfloat16)
    quant = jnp.transpose(quant, (1, 0, 2))
    blocks = quant.reshape(2, PAGES, PAGE, width)
    block_ids = jnp.arange(PAGES, dtype=jnp.int32)
    target = block_ids // PAGES_DEV * PAGES_DEV + page_table
    kv_cache = jnp.zeros((2, PAGES, PAGE, width), jnp.bfloat16).at[:, target].set(blocks)
    total_rows = STEPS * ROWS
    query_rows = queries.reshape(total_rows, KVH, GROUP, HD)
    own_keys = new_keys.reshape(total_rows, KVH, HD)
    own_values = new_values.reshape(total_rows, KVH, HD)
    row_pos = positions.reshape(total_rows)
    row_prompt = jnp.arange(total_rows, dtype=jnp.int32) % ROWS // (ROWS // 2)
    mask = (prompt_of[None, :] == row_prompt[:, None]) & (place[None, :] < row_pos[:, None])
    keys_all = quant[0].reshape(TOKENS, KVH, HD)
    values_all = quant[1].reshape(TOKENS, KVH, HD)
    key_scales = scales[0].reshape(KVH, HD)
    value_scales = scales[1].reshape(KVH, HD)
    inverse = 1.0 / jnp.sqrt(jnp.float32(HD))

    def one_head(head):
        query_head = query_rows[:, head].astype(jnp.float32)
        scaled = (query_head * key_scales[head][None, None, :]).astype(jnp.bfloat16)
        keys_head = keys_all[:, head]
        values_head = values_all[:, head]
        score = jnp.einsum('rgd,kd->rgk', scaled.astype(jnp.float32), keys_head.astype(jnp.float32)) * inverse
        own = jnp.einsum('rgd,rd->rg', query_head, own_keys[:, head].astype(jnp.float32)) * inverse
        held = jnp.where(mask[:, None, :], score, masked_fill)
        top = jnp.maximum(lax.optimization_barrier(jnp.max(held, axis=-1)), own)
        weight = jnp.where(mask[:, None, :], jnp.exp(score - top[..., None]), 0.0)
        own_weight = jnp.exp(own - top)
        total = lax.optimization_barrier(jnp.sum(weight, axis=-1)) + own_weight
        rounded = weight.astype(jnp.bfloat16)
        summed = jnp.einsum('rgk,kd->rgd', rounded.astype(jnp.float32), values_head.astype(jnp.float32))
        result = summed * value_scales[head][None, None, :] + own_weight[..., None] * own_values[:, head][:, None, :].astype(jnp.float32)
        return result / total[..., None]
    outputs = lax.map(one_head, jnp.arange(KVH, dtype=jnp.int32))
    attended = jnp.transpose(outputs, (1, 0, 2, 3)).reshape(STEPS, ROWS, QH * HD).astype(jnp.bfloat16)
    return (kv_cache, scales, attended)
```

```python
import functools

import jax
import jax.numpy as jnp
from jax import lax
from jax.experimental import pallas as pl
from jax.experimental.pallas import tpu as pltpu
from jax.sharding import Mesh, PartitionSpec as P

HD = 128
PAGE = 256
PIECE = 256
TILE = 320
GROUP = 8

eps = 1e-05
clip_level = 2.5
masked_fill = -1e30
inverse = 1.0 / (float(HD) ** 0.5)

SIZES = {"yh": 2, "z": 8, "tp": 2, "x": 4, "core": 2}


def shift(value, axis, step):
    n = SIZES[axis]
    return lax.ppermute(value, axis, [(i, (i + step) % n) for i in range(n)])


def project_kernel(n, tiles, has_acc, last, s_ref, *refs):
    own, sib, weights = refs[:n], refs[n : 2 * n], refs[2 * n : 3 * n]
    refs = refs[3 * n :]
    acc = None
    if has_acc:
        acc, refs = refs[0], refs[1:]
    out = refs[0]
    step = pl.program_id(0)
    weight = jnp.concatenate([w[...] for w in weights], axis=0)

    def work(tokens):
        rows = jnp.concatenate([t[...] for t in tokens], axis=1)
        value = jnp.dot(rows, weight, preferred_element_type=jnp.float32)
        if has_acc:
            value = value + acc[...]
        out[...] = value
        if last:
            squares = refs[1]
            side = step // tiles
            start = jnp.where(side == 0, s_ref[n], s_ref[n + 1]) + (step % tiles) * TILE
            place = start + lax.broadcasted_iota(jnp.int32, value.shape, 0)
            kept = jnp.where(place < s_ref[n + 2], value * value, 0.0)
            part = jnp.sum(kept, axis=0, keepdims=True)[None]
            part = jnp.broadcast_to(part, squares.shape)

            @pl.when(step == 0)
            def _():
                squares[...] = part

            @pl.when(step > 0)
            def _():
                squares[...] += part

    @pl.when(step < tiles)
    def _():
        work(own)

    @pl.when(step >= tiles)
    def _():
        work(sib)


def project(own, sib, pieces, ids, acc=None, last=None):
    n = len(pieces)
    rows = own.shape[0]
    tiles = rows // TILE
    width = pieces[0].shape[1]
    scalars = jnp.stack(list(ids) + (list(last) if last is not None else [])).astype(jnp.int32)
    in_specs = []
    for i in range(n):
        in_specs.append(
            pl.BlockSpec((TILE, PIECE), lambda g, s, i=i: (jnp.minimum(g, tiles - 1), s[i]))
        )
    for i in range(n):
        in_specs.append(
            pl.BlockSpec((TILE, PIECE), lambda g, s, i=i: (jnp.maximum(g - tiles, 0), s[i]))
        )
    for i in range(n):
        in_specs.append(pl.BlockSpec((PIECE, width), lambda g, s: (0, 0)))
    args = [own] * n + [sib] * n + list(pieces)
    aliases = {}
    if acc is not None:
        in_specs.append(pl.BlockSpec((TILE, width), lambda g, s: (g, 0)))
        aliases = {1 + len(args): 0}
        args.append(acc)
    out_shape = [jax.ShapeDtypeStruct((2 * rows, width), jnp.float32)]
    out_specs = [pl.BlockSpec((TILE, width), lambda g, s: (g, 0))]
    if last is not None:
        out_shape.append(jax.ShapeDtypeStruct((64, 1, width), jnp.float32))
        out_specs.append(pl.BlockSpec((64, 1, width), lambda g, s: (0, 0, 0)))
    return pl.pallas_call(
        functools.partial(project_kernel, n, tiles, acc is not None, last is not None),
        grid_spec=pltpu.PrefetchScalarGridSpec(
            num_scalar_prefetch=1, grid=(2 * tiles,), in_specs=in_specs, out_specs=out_specs
        ),
        out_shape=out_shape,
        input_output_aliases=aliases,
        compiler_params=pltpu.CompilerParams(vmem_limit_bytes=32 * 1024 * 1024),
        cost_estimate=pl.CostEstimate(
            flops=2 * 2 * rows * PIECE * n * width,
            bytes_accessed=2 * rows * PIECE * n * 2 + n * PIECE * width * 2 + 16 * rows * width,
            transcendentals=0,
        ),
    )(scalars, *args)


def quantize_kernel(s_ref, proj, squares, count, *outs):
    scale = jnp.sqrt(jnp.sum(squares[:, 0, :], axis=0, keepdims=True) / count[0, 0] + eps)
    outs[4][...] = scale
    value = jnp.clip(proj[...] / scale, -clip_level, clip_level).astype(jnp.bfloat16)
    for k in range(4):
        for i in range(4):

            @pl.when(s_ref[1 + k] == i)
            def _(k=k, i=i):
                outs[k][...] = value[:, i * HD : (i + 1) * HD]


def quantize(proj, squares, count, scalars):
    rows, width = proj.shape
    half = rows // 2
    place = lambda g, s: (jnp.where(s[0] == 0, g, 1 - g), 0)
    return pl.pallas_call(
        quantize_kernel,
        grid_spec=pltpu.PrefetchScalarGridSpec(
            num_scalar_prefetch=1,
            grid=(2,),
            in_specs=[
                pl.BlockSpec((half, width), lambda g, s: (g, 0)),
                pl.BlockSpec(squares.shape, lambda g, s: (0, 0, 0)),
                pl.BlockSpec(memory_space=pltpu.SMEM),
            ],
            out_specs=[pl.BlockSpec((half, HD), place)] * 4
            + [pl.BlockSpec((1, width), lambda g, s: (0, 0))],
        ),
        out_shape=[jax.ShapeDtypeStruct((rows, HD), jnp.bfloat16)] * 4
        + [jax.ShapeDtypeStruct((1, width), jnp.float32)],
        compiler_params=pltpu.CompilerParams(vmem_limit_bytes=32 * 1024 * 1024),
        cost_estimate=pl.CostEstimate(
            flops=4 * rows * width, bytes_accessed=6 * rows * width, transcendentals=0
        ),
    )(scalars, proj, squares, count)


def attend_kernel(s_ref, r0, r1, r2, r3, query, limits, key_scale, cache, part, held, sems):
    got = (r0, r1, r2, r3)
    rows = r0.shape[0]
    for m in range(4):

        @pl.when(s_ref[0] == m)
        def _(m=m):
            for j in range(4):
                held[j // 2, pl.ds((j % 2) * rows, rows)] = got[(m - j) % 4][...]

    pages = 2 * rows // PAGE
    copies = []
    for j in range(2):
        for b in range(pages):
            copies.append(
                pltpu.make_async_copy(
                    held.at[j, pl.ds(b * PAGE, PAGE)], cache.at[j, s_ref[2 + b]], sems.at[j, b]
                )
            )
    for copy in copies:
        copy.start()
    keys, values = held[0], held[1]
    block = 128
    for at in range(0, query.shape[0], block):
        piece = pl.ds(at, block)
        scaled = (query[piece].astype(jnp.float32) * key_scale[...]).astype(jnp.bfloat16)
        score = (
            lax.dot_general(
                scaled, keys, (((1,), (1,)), ((), ())), preferred_element_type=jnp.float32
            )
            * inverse
        )
        place = s_ref[1] + lax.broadcasted_iota(jnp.int32, score.shape, 1)
        score = jnp.where(place < limits[piece], score, masked_fill)
        top = jnp.max(score, axis=1, keepdims=True)
        weight = jnp.where(score > 0.5 * masked_fill, jnp.exp(score - top), 0.0)
        total = jnp.sum(weight, axis=1, keepdims=True)
        part[piece, :HD] = jnp.dot(
            weight.astype(jnp.bfloat16), values, preferred_element_type=jnp.float32
        )
        part[piece, HD : HD + 64] = jnp.broadcast_to(top, (block, 64))
        part[piece, HD + 64 :] = jnp.broadcast_to(total, (block, 64))
    for copy in copies:
        copy.wait()


def attend(received, query, limits, key_scale, scalars):
    rows = received[0].shape[0]
    pages = 2 * rows // PAGE
    heads = query.shape[0]
    whole = pl.BlockSpec(memory_space=pltpu.VMEM)
    return pl.pallas_call(
        attend_kernel,
        grid_spec=pltpu.PrefetchScalarGridSpec(
            num_scalar_prefetch=1,
            grid=(),
            in_specs=[whole] * 7,
            out_specs=[pl.BlockSpec(memory_space=pl.ANY), whole],
            scratch_shapes=[
                pltpu.VMEM((2, 2 * rows, HD), jnp.bfloat16),
                pltpu.SemaphoreType.DMA((2, pages)),
            ],
        ),
        out_shape=[
            jax.ShapeDtypeStruct((2, pages, PAGE, HD), jnp.bfloat16),
            jax.ShapeDtypeStruct((heads, 2 * HD), jnp.float32),
        ],
        compiler_params=pltpu.CompilerParams(vmem_limit_bytes=40 * 1024 * 1024),
        cost_estimate=pl.CostEstimate(
            flops=8 * heads * rows * HD,
            bytes_accessed=16 * rows * HD,
            transcendentals=2 * heads * rows,
        ),
    )(scalars, *received, query, limits, key_scale)


def merge_kernel(parts, query, new_key, new_value, value_scale, out):
    top = parts[:, :, HD : HD + 1]
    total = parts[:, :, HD + 64 : HD + 65]
    own = (
        jnp.sum(
            query[...].astype(jnp.float32) * new_key[...].astype(jnp.float32), axis=1, keepdims=True
        )
        * inverse
    )
    overall = jnp.maximum(jnp.max(top, axis=0), own)
    factor = jnp.exp(top - overall[None])
    own_weight = jnp.exp(own - overall)
    denominator = jnp.sum(total * factor, axis=0) + own_weight
    summed = jnp.sum(parts[:, :, :HD] * factor, axis=0)
    result = summed * value_scale[...] + own_weight * new_value[...].astype(jnp.float32)
    result = (result / denominator).astype(out.dtype)
    out[...] = jnp.broadcast_to(result[None], out.shape)


def merge(parts, query, new_key, new_value, value_scale):
    whole = pl.BlockSpec(memory_space=pltpu.VMEM)
    return pl.pallas_call(
        merge_kernel,
        in_specs=[whole] * 5,
        out_specs=whole,
        out_shape=jax.ShapeDtypeStruct((32,) + query.shape, jnp.bfloat16),
        cost_estimate=pl.CostEstimate(flops=1 << 18, bytes_accessed=1 << 19, transcendentals=512),
    )(parts, query, new_key, new_value, value_scale)


def body(tokens, kv_weight, lengths, page_table, queries, new_keys, new_values, positions):
    yh, z = lax.axis_index("yh"), lax.axis_index("z")
    tp, x, core = lax.axis_index("tp"), lax.axis_index("x"), lax.axis_index("core")
    rows = tokens.shape[0]
    parity = x % 2
    sibling = lax.ppermute(tokens, "core", [(0, 1), (1, 0)])

    def half(which):
        return jnp.concatenate(
            [
                lax.dynamic_slice(kv_weight, (which * PIECE, (2 * i + core) * HD), (PIECE, HD))
                for i in range(4)
            ],
            axis=1,
        )

    first, second = half(parity), half(1 - parity)

    def ident(other, dz, mine):
        return (((yh + other) % 2) * 8 + (z + dz) % 8) * 2 + (parity if mine else 1 - parity)

    waves = [[(first, ident(0, 0, True)), (second, ident(0, 0, False))]]

    def arrived(value, other, dz, way, wave):
        wave.append((value, ident(other, dz, True)))
        wave.append((shift(value, "x", way), ident(other, dz, False)))

    wave = []
    cross = shift(first, "yh", 1)
    arrived(cross, 1, 0, 1, wave)
    pa, ma, pb, mb = first, first, cross, cross
    for j in (1, 2):
        pa, ma = shift(pa, "z", 1), shift(ma, "z", -1)
        pb, mb = shift(pb, "z", 1), shift(mb, "z", -1)
        arrived(pa, 0, -j, -1, wave)
        arrived(ma, 0, j, 1, wave)
        arrived(pb, 1, -j, -1, wave)
        arrived(mb, 1, j, 1, wave)
        waves.append(wave)
        wave = []
    pa, ma = shift(pa, "z", 1), shift(ma, "z", -1)
    arrived(pa, 0, -3, -1, wave)
    arrived(ma, 0, 3, 1, wave)
    arrived(shift(pa, "yh", 1), 1, -3, -1, wave)
    arrived(shift(ma, "yh", 1), 1, 3, 1, wave)
    waves.append(wave)
    wave = []
    pa = shift(pa, "z", 1)
    arrived(pa, 0, 4, -1, wave)
    arrived(shift(pa, "yh", 1), 1, 4, 1, wave)
    waves.append(wave)

    source = (z * 8 + 2 * x) * rows
    limit = jnp.where(yh == 0, lengths[0], lengths[1])
    acc = None
    for w, wave in enumerate(waves):
        last = None
        if w == len(waves) - 1:
            last = (source + core * rows, source + (1 - core) * rows, limit)
        done = project(tokens, sibling, [p for p, _ in wave], [i for _, i in wave], acc, last)
        acc = done[0]
    squares = lax.all_to_all(done[1], ("yh", "z", "x"), 0, 0, tiled=True)

    count = (lengths[0] + lengths[1]).astype(jnp.float32).reshape(1, 1)
    scalars = jnp.stack([core] + [(x + k + 2 * tp) % 4 for k in range(4)]).astype(jnp.int32)
    *sent, scale = quantize(acc, squares, count, scalars)

    received = []
    for k in range(4):
        pairs = []
        for t in range(2):
            for a in range(4):
                pairs.append((t * 4 + a, (a // 2) * 4 + (a + k + 2 * t) % 4))
        received.append(lax.ppermute(sent[k], ("tp", "x"), pairs))

    other_scale = shift(scale, "tp", 1)
    both = jnp.where(
        tp == 0,
        jnp.concatenate([scale, other_scale], axis=0),
        jnp.concatenate([other_scale, scale], axis=0),
    )
    head_scales = lax.dynamic_slice(both, (0, x * HD), (2, HD))
    far = shift(both, "core", 1)
    pair = jnp.where(
        core == 0,
        jnp.stack([both.reshape(2, 4, HD), far.reshape(2, 4, HD)], axis=2),
        jnp.stack([far.reshape(2, 4, HD), both.reshape(2, 4, HD)], axis=2),
    )
    scales = pair.reshape(2, 8 * HD)

    query = lax.dynamic_slice(queries, (0, 32 * yh, 0), (2, 32, GROUP * HD)).reshape(512, HD)
    limits = lax.dynamic_slice(positions, (0, 32 * yh), (2, 32)).reshape(64, 1)
    limits = jnp.broadcast_to(limits, (64, GROUP)).reshape(512, 1)
    place = z * 2 + tp
    scalars = jnp.concatenate(
        [jnp.stack([(x - 2 * tp) % 4, place * 4 * rows]).astype(jnp.int32), page_table]
    )
    kv_cache, part = attend(received, query, limits, head_scales[:1], scalars)
    parts = lax.all_to_all(part.reshape(16, 32, 2 * HD), ("z", "tp"), 0, 0, tiled=True)

    mine = lax.dynamic_slice(query, (place * 32, 0), (32, HD))
    at = (place // 8, yh * 32 + (place % 8) * 4, 0)

    def spread(array):
        rows_here = lax.dynamic_slice(array, at, (1, 4, HD)).reshape(4, 1, HD)
        return jnp.broadcast_to(rows_here, (4, GROUP, HD)).reshape(32, HD)

    result = merge(parts, mine, spread(new_keys), spread(new_values), head_scales[1:])
    whole = lax.all_to_all(result, ("yh", "z", "tp"), 0, 0, tiled=True)
    whole = whole.reshape(2, 2, 32, GROUP * HD)
    attended = jnp.transpose(whole, (1, 0, 2, 3)).reshape(2, 64, GROUP * HD)
    return (kv_cache, scales, attended)


def solution(mesh):
    names = tuple(SIZES)
    fine = Mesh(mesh.devices.reshape(tuple(SIZES.values())), names)
    seq, head = ("yh", "z"), ("x", "core")
    in_specs = (
        P(seq + head, None),
        P(seq, "tp"),
        P(),
        P(seq + ("tp",)),
        P(None, None, head),
        P(None, None, head),
        P(None, None, head),
        P(),
    )
    out_specs = (P(None, seq + ("tp",), None, head), P(), P(None, None, head))
    return jax.shard_map(body, mesh=fine, in_specs=in_specs, out_specs=out_specs, check_vma=False)
```

```python
import functools
import math

import jax
import jax.numpy as jnp
from jax import lax
from jax.experimental import pallas as pl
from jax.experimental.pallas import tpu as pltpu
from jax.sharding import Mesh, PartitionSpec as P

HD = 128
PAGE = 256
PIECE = 256
TILE = 320
GROUP = 8
MIB = 1024 * 1024
VMEM = 60 * MIB
SHARED = 16 * MIB

eps = 1e-05
clip_level = 2.5
masked_fill = -1e30
inverse = 1.0 / (float(HD) ** 0.5)

SIZES = {"yh": 2, "z": 8, "tp": 2, "x": 4, "core": 2}
ANYWHERE = pl.BlockSpec(memory_space=pl.ANY)
WHOLE = pl.BlockSpec(memory_space=pltpu.VMEM)
SCALAR = pl.BlockSpec(memory_space=pltpu.SMEM)


def params(limit):
    return pltpu.CompilerParams(vmem_limit_bytes=limit)


def cost(flops=0, size=0, exps=0):
    return pl.CostEstimate(flops=flops, bytes_accessed=size, transcendentals=exps)


def send(value, **steps):
    names = tuple(steps)
    sizes = [SIZES[name] for name in names]
    pairs = []
    for i in range(math.prod(sizes)):
        target, rest = 0, i
        place = []
        for n in reversed(sizes):
            place.insert(0, rest % n)
            rest //= n
        for at, n, name in zip(place, sizes, names):
            target = target * n + (at + steps[name]) % n
        pairs.append((i, target))
    return lax.ppermute(value, names if len(names) > 1 else names[0], pairs)


def gate_kernel(*refs):
    pass


def gate(values, after):
    args = [pltpu.with_memory_space_constraint(v, pltpu.HBM) for v in values]
    return pl.pallas_call(
        gate_kernel,
        in_specs=[ANYWHERE] * (len(args) + 1),
        out_specs=[ANYWHERE] * len(args),
        out_shape=[jax.ShapeDtypeStruct(v.shape, v.dtype) for v in values],
        input_output_aliases={i: i for i in range(len(args))},
        compiler_params=params(SHARED),
        cost_estimate=cost(),
    )(*args, after)


def keep_kernel(source, target, sem):
    copy = pltpu.make_async_copy(source, target, sem)
    copy.start()
    copy.wait()


def keep(value):
    return pl.pallas_call(
        keep_kernel,
        in_specs=[ANYWHERE],
        out_specs=ANYWHERE,
        out_shape=pltpu.VMEM(value.shape, value.dtype),
        scratch_shapes=[pltpu.SemaphoreType.DMA],
        compiler_params=params(SHARED),
        cost_estimate=cost(size=2 * value.size * value.dtype.itemsize),
    )(value)


def take_kernel(weight, out, sems):
    core, half = lax.axis_index("core"), lax.axis_index("x") % 2
    copies = []
    for i in range(4):
        copies.append(
            pltpu.make_async_copy(
                weight.at[
                    pl.ds(pl.multiple_of(half * PIECE, PIECE), PIECE),
                    pl.ds(pl.multiple_of((2 * i + core) * HD, HD), HD),
                ],
                out.at[:, pl.ds(i * HD, HD)],
                sems.at[i],
            )
        )
    for copy in copies:
        copy.start()
    for copy in copies:
        copy.wait()


def take(weight):
    return pl.pallas_call(
        take_kernel,
        in_specs=[ANYWHERE],
        out_specs=ANYWHERE,
        out_shape=pltpu.HBM((PIECE, 4 * HD), weight.dtype),
        scratch_shapes=[pltpu.SemaphoreType.DMA((4,))],
        compiler_params=params(SHARED),
        cost_estimate=cost(size=MIB),
    )(weight)


def project_kernel(names, has_acc, last, own, sib, *refs):
    arrays = len(names)
    sources, refs = refs[:arrays], refs[arrays:]
    acc = lengths = None
    if has_acc:
        acc, refs = refs[0], refs[1:]
    if last:
        lengths, refs = refs[0], refs[1:]
    outs, (held, sems) = refs[:-2], refs[-2:]
    yh, z, x = lax.axis_index("yh"), lax.axis_index("z"), lax.axis_index("x")
    core = lax.axis_index("core")
    width = held.shape[1]
    copies, columns, sem = [], [], 0
    for i, pieces in enumerate(names):
        at = len(columns) * PIECE
        if pieces is None:
            pieces = [(0, 0, None), (0, 0, None)]
            some = [
                pltpu.make_async_copy(
                    sources[i].at[:, pl.ds(pl.multiple_of((2 * j + core) * HD, HD), HD)],
                    held.at[pl.ds(at, 2 * PIECE), pl.ds(j * HD, HD)],
                    sems.at[sem + j],
                )
                for j in range(4)
            ]
        else:
            some = [
                pltpu.make_async_copy(
                    sources[i], held.at[pl.ds(at, len(pieces) * PIECE)], sems.at[sem]
                )
            ]
        sem += len(some)
        for j, (other, dz, mine) in enumerate(pieces):
            half = j if mine is None else (x + (0 if mine else 1)) % 2
            shard = ((yh + other) % 2) * 8 + (z + dz + 8) % 8
            columns.append(pl.multiple_of((shard * 2 + half) * PIECE, PIECE))
            copies.append(some if j == 0 else [])
    for some in copies:
        for copy in some:
            copy.start()
    rows = own.shape[0]
    total = refs[-3] if last else outs[0]
    for piece, column in enumerate(columns):
        for copy in copies[piece]:
            copy.wait()
        weight = held[piece * PIECE : (piece + 1) * PIECE]
        for side, tokens in enumerate((own, sib)):
            for row in range(0, rows, TILE):
                value = jnp.dot(
                    tokens[pl.ds(row, TILE), pl.ds(column, PIECE)],
                    weight,
                    preferred_element_type=jnp.float32,
                )
                here = pl.ds(side * rows + row, TILE)
                if piece > 0:
                    total[here] += value
                elif has_acc:
                    total[here] = acc[here] + value
                else:
                    total[here] = value
    if not last:
        return
    squares = outs[1]
    part = jnp.zeros((1, width), jnp.float32)
    limit = jnp.where(yh == 0, lengths[0], lengths[1])
    for row in range(0, 2 * rows, TILE):
        value = total[row : row + TILE]
        goes = pl.multiple_of((row + core * rows) % (2 * rows), TILE)
        place = (z * 4 + x) * 2 * rows + goes + lax.broadcasted_iota(jnp.int32, value.shape, 0)
        kept = jnp.where(place < limit, value * value, 0.0)
        part = part + jnp.sum(kept, axis=0, keepdims=True)
        outs[0][pl.ds(goes, TILE)] = value
    squares[...] = jnp.broadcast_to(part[None], squares.shape)


def project(own, sib, pieces, acc=None, lengths=None):
    names = [ids for _, ids in pieces]
    n = sum(2 if ids is None else len(ids) for ids in names)
    rows, width = own.shape[0], 4 * HD
    last = lengths is not None
    in_specs = [WHOLE, WHOLE] + [ANYWHERE] * len(pieces)
    args = [pltpu.with_memory_space_constraint(value, pltpu.VMEM) for value in (own, sib)]
    args += [pltpu.with_memory_space_constraint(value, pltpu.HBM) for value, _ in pieces]
    aliases = {}
    if acc is not None:
        in_specs.append(WHOLE)
        if not last:
            aliases = {len(args): 0}
        args.append(acc)
    scratch = [
        pltpu.VMEM((n * PIECE, width), jnp.bfloat16),
        pltpu.SemaphoreType.DMA((len(pieces) + 3,)),
    ]
    if not last:
        out_shape = [pltpu.VMEM((2 * rows, width), jnp.float32)]
    else:
        in_specs.append(SCALAR)
        args.append(lengths)
        out_shape = [pltpu.VMEM((2 * rows, width), jnp.float32)]
        out_shape.append(jax.ShapeDtypeStruct((64, 1, width), jnp.float32))
        scratch.insert(0, pltpu.VMEM((2 * rows, width), jnp.float32))
    return pl.pallas_call(
        functools.partial(project_kernel, names, acc is not None, last),
        in_specs=in_specs,
        out_specs=[WHOLE] * len(out_shape),
        scratch_shapes=scratch,
        out_shape=out_shape,
        input_output_aliases=aliases,
        compiler_params=params(SHARED),
        cost_estimate=cost(4 * rows * PIECE * n * width, n * PIECE * width * 2),
    )(*args)


def quantize_kernel(proj, squares, lengths, *outs):
    x, tp = lax.axis_index("x"), lax.axis_index("tp")
    count = (lengths[0] + lengths[1]).astype(jnp.float32)
    scale = jnp.sqrt(jnp.sum(squares[:, 0, :], axis=0, keepdims=True) / count + eps)
    outs[4][...] = scale
    for k in range(4):
        head = pl.ds(pl.multiple_of(((x + k + 2 * tp) % 4) * HD, HD), HD)
        value = proj[:, head] * (1.0 / outs[4][:, head])
        outs[k][...] = jnp.clip(value, -clip_level, clip_level).astype(jnp.bfloat16)


def quantize(proj, squares, lengths):
    rows, width = proj.shape
    return pl.pallas_call(
        quantize_kernel,
        in_specs=[WHOLE, WHOLE, SCALAR],
        out_specs=[WHOLE] * 5,
        out_shape=[jax.ShapeDtypeStruct((rows, HD), jnp.bfloat16)] * 4
        + [jax.ShapeDtypeStruct((1, width), jnp.float32)],
        compiler_params=params(54 * MIB),
        cost_estimate=cost(4 * rows * width, 6 * rows * width),
    )(proj, squares, lengths)


def head_scale(own, other, side):
    here = pl.ds(pl.multiple_of(lax.axis_index("x") * HD, HD), HD)
    return jnp.where(lax.axis_index("tp") == side, own[:, here], other[:, here])


def attend_kernel(
    pages, r0, r1, r2, r3, query, limits, own_scale, other_scale, cache, part, held, tops, totals, sems
):
    yh, z, x, tp = [lax.axis_index(name) for name in ("yh", "z", "x", "tp")]
    got = (r0, r1, r2, r3)
    rows = r0.shape[0]
    scales = [head_scale(own_scale, other_scale, side) for side in range(2)]
    first = (x - 2 * tp + 4) % 4
    for m in range(4):

        @pl.when(first == m)
        def _(m=m):
            for j in range(4):
                held[j // 2, pl.ds((j % 2) * rows, rows)] = got[(m - j) % 4][...]

    count = 2 * rows // PAGE
    copies = []
    for j in range(2):
        for b in range(count):
            copies.append(
                pltpu.make_async_copy(
                    held.at[j, pl.ds(b * PAGE, PAGE)], cache.at[j, pages[b]], sems.at[j, b]
                )
            )
    for copy in copies:
        copy.start()
    keys, values = held[0], held[1]
    seen = pl.multiple_of(yh * 32, 32)
    limit = jnp.concatenate([limits[pl.ds(s * 64 + seen, 32)] for s in range(2)], axis=0)
    limit = jnp.concatenate([limit, limit], axis=0)
    base = (z * 2 + tp) * 2 * rows
    for pair in range(GROUP // 2):
        asked = [
            query[s, pl.ds(seen, 32), g * HD : (g + 1) * HD]
            for g in (2 * pair, 2 * pair + 1)
            for s in range(2)
        ]
        asked = jnp.concatenate(asked, axis=0)
        scaled = (asked.astype(jnp.float32) * scales[0]).astype(jnp.bfloat16)
        score = (
            lax.dot_general(
                scaled, keys, (((1,), (1,)), ((), ())), preferred_element_type=jnp.float32
            )
            * inverse
        )
        mask = base + lax.broadcasted_iota(jnp.int32, score.shape, 1) < limit
        top = jnp.max(jnp.where(mask, score, masked_fill), axis=1, keepdims=True)
        weight = jnp.where(mask, jnp.exp(score - top), 0.0)
        total = jnp.sum(weight, axis=1, keepdims=True)
        summed = jnp.dot(weight.astype(jnp.bfloat16), values, preferred_element_type=jnp.float32)
        for side in range(2):
            g = 2 * pair + side
            for block in range(8):
                source = slice(side * 64 + block * 8, side * 64 + block * 8 + 8)
                target = 2 * block + g // 4, slice((g % 4) * 8, (g % 4) * 8 + 8)
                part[target] = summed[source]
                tops[target], totals[target] = [
                    jnp.broadcast_to(value[source], (8, HD)) for value in (top, total)
                ]
    here = lax.broadcasted_iota(jnp.int32, (32, HD), 0) == lax.broadcasted_iota(
        jnp.int32, (32, HD), 1
    )
    for share in range(16):
        for at, column in enumerate((tops, totals)):
            part[share, 32 + at : 33 + at] = jnp.sum(
                jnp.where(here, column[share], 0.0), axis=0, keepdims=True
            )
    for copy in copies:
        copy.wait()


def attend(received, query, limits, own_scale, other_scale, page_table):
    rows = received[0].shape[0]
    pages = 2 * rows // PAGE
    heads = 512
    return pl.pallas_call(
        attend_kernel,
        in_specs=[SCALAR] + [WHOLE] * 8,
        out_specs=[ANYWHERE, WHOLE],
        scratch_shapes=[
            pltpu.VMEM((2, 2 * rows, HD), jnp.bfloat16),
            pltpu.VMEM((16, 32, HD), jnp.float32),
            pltpu.VMEM((16, 32, HD), jnp.float32),
            pltpu.SemaphoreType.DMA((2, pages)),
        ],
        out_shape=[
            jax.ShapeDtypeStruct((2, pages, PAGE, HD), jnp.bfloat16),
            jax.ShapeDtypeStruct((16, 40, HD), jnp.float32),
        ],
        compiler_params=params(VMEM),
        cost_estimate=cost(8 * heads * rows * HD, 16 * rows * HD, 2 * heads * rows),
    )(page_table, *received, query, limits, own_scale, other_scale)


def merge_kernel(parts, query, new_key, new_value, own_scale, other_scale, out, rows):
    yh, z, tp = [lax.axis_index(name) for name in ("yh", "z", "tp")]
    seen = pl.multiple_of(yh * 32, 32)
    step, at = z // 4, pl.multiple_of((z % 4) * 8, 8)
    half = 4 * HD
    rows[:, :half] = query[step, pl.ds(seen, 32), pl.ds(pl.multiple_of(tp * half, half), half)].astype(
        jnp.float32
    )
    rows[:, half : half + HD] = new_key[step, pl.ds(seen, 32)].astype(jnp.float32)
    rows[:, half + HD :] = new_value[step, pl.ds(seen, 32)].astype(jnp.float32)
    key = rows[pl.ds(at, 8), half : half + HD]
    value = rows[pl.ds(at, 8), half + HD :]
    scale = head_scale(own_scale, other_scale, 1)
    own = [
        jnp.sum(rows[pl.ds(at, 8), g * HD : (g + 1) * HD] * key, axis=1, keepdims=True) * inverse
        for g in range(4)
    ]
    own = jnp.concatenate(own, axis=0)
    value = jnp.concatenate([value] * 4, axis=0)
    here = lax.broadcasted_iota(jnp.int32, (1, 32, HD), 1) == lax.broadcasted_iota(
        jnp.int32, (1, 32, HD), 2
    )
    top, total = [
        jnp.sum(jnp.where(here, parts[:, at : at + 1, :], 0.0), axis=2, keepdims=True)
        for at in (32, 33)
    ]
    overall = jnp.maximum(jnp.max(top, axis=0), own)
    factor = jnp.exp(top - overall[None])
    own_weight = jnp.exp(own - overall)
    denominator = jnp.sum(total * factor, axis=0) + own_weight
    summed = jnp.sum(parts[:, :32, :] * factor, axis=0)
    result = (summed * scale + own_weight * value) / denominator
    out[...] = jnp.broadcast_to(result.astype(out.dtype)[None], out.shape)


def merge(parts, query, new_key, new_value, own_scale, other_scale):
    return pl.pallas_call(
        merge_kernel,
        in_specs=[WHOLE] * 6,
        out_specs=WHOLE,
        out_shape=jax.ShapeDtypeStruct((32, 32, HD), jnp.bfloat16),
        scratch_shapes=[pltpu.VMEM((32, 6 * HD), jnp.float32)],
        compiler_params=params(VMEM),
        cost_estimate=cost(1 << 18, 1 << 19, 512),
    )(parts, query, new_key, new_value, own_scale, other_scale)


def finish_kernel(whole, both, far, attended, scales):
    for yh in range(2):
        for step in range(2):
            for side in range(2):
                blocks = [
                    whole[yh * 16 + 2 * (step * 4 + part) + side].astype(jnp.float32)
                    for part in range(4)
                ]
                for g in range(4):
                    value = jnp.concatenate([b[g * 8 : g * 8 + 8] for b in blocks], axis=0)
                    head = side * 4 + g
                    attended[step, yh * 32 : yh * 32 + 32, head * HD : (head + 1) * HD] = (
                        value.astype(attended.dtype)
                    )
    tp, core = lax.axis_index("tp"), lax.axis_index("core")
    for side in range(2):
        for i in range(4):
            lanes = slice(i * HD, (i + 1) * HD)
            for c in range(2):
                own = jnp.where(core == c, both[0:1, lanes], far[0:1, lanes])
                other = jnp.where(core == c, both[1:2, lanes], far[1:2, lanes])
                scales[side : side + 1, (2 * i + c) * HD : (2 * i + c + 1) * HD] = jnp.where(
                    tp == side, own, other
                )


def finish(whole, both, far):
    return pl.pallas_call(
        finish_kernel,
        in_specs=[WHOLE] * 3,
        out_specs=[WHOLE] * 2,
        out_shape=[
            jax.ShapeDtypeStruct((2, 64, GROUP * HD), jnp.bfloat16),
            jax.ShapeDtypeStruct((2, 8 * HD), jnp.float32),
        ],
        compiler_params=params(VMEM),
        cost_estimate=cost(0, MIB // 2),
    )(whole, both, far)


def body(tokens, kv_weight, lengths, page_table, queries, new_keys, new_values, positions):
    sibling = send(tokens, core=1)
    own = keep(pltpu.with_memory_space_constraint(tokens, pltpu.HBM))

    def joined(*values):
        return jnp.concatenate(values, axis=0)

    def swapped(ids):
        return [(other, dz, False) for other, dz, _ in ids]

    first = take(kv_weight)
    cross = send(first, yh=1)
    up, down = send(first, z=1), send(first, z=-1)
    up_far, down_far = send(first, yh=1, z=1), send(first, yh=1, z=-1)
    cross, up, up_far, down, down_far = gate([cross, up, up_far, down, down_far], own)
    up, down = joined(up, up_far), joined(down, down_far)
    at = lambda dz: [(0, dz, True), (1, dz, True)]

    sides = send(cross, x=1), send(up, x=-1), send(down, x=1)
    next_up, next_down = send(up, z=1), send(down, z=-1)
    sib = keep(sibling)
    next_up, next_down, *sides = gate([next_up, next_down, *sides], sib)
    wave = [(kv_weight, None), (cross, [(1, 0, True)]), (up, at(-1)), (down, at(1))]
    wave += [(sides[0], [(1, 0, False)]), (sides[1], swapped(at(-1))), (sides[2], swapped(at(1)))]
    wave += [(next_up, at(-2)), (next_down, at(2))]
    up, down = next_up, next_down

    acc = project(own, sib, wave)[0]
    sides = send(up, x=-1), send(down, x=1)
    next_up, next_down = send(up, z=1), send(down, z=-1)
    next_up, next_down, *sides = gate([next_up, next_down, *sides], acc)
    wave = [(next_up, at(-3)), (next_down, at(3))]
    wave += [(sides[0], swapped(at(-2))), (sides[1], swapped(at(2)))]
    up, down = next_up, next_down

    near, far = up[:PIECE], down[PIECE:]
    wave_last = [(send(near, z=1), at(-4)[:1]), (send(far, z=-1), at(4)[1:])]
    wave_last += [(send(up, x=-1), swapped(at(-3))), (send(down, x=1), swapped(at(3)))]
    wave_last += [(send(near, z=1, x=-1), swapped(at(-4)[:1]))]
    wave_last += [(send(far, z=-1, x=1), swapped(at(4)[1:]))]
    acc = project(own, sib, wave, acc)[0]
    proj, squares = project(own, sib, wave_last, acc, lengths)
    squares = lax.all_to_all(squares, ("yh", "z", "x"), 0, 0, tiled=True)
    *sent, scale = quantize(proj, squares, lengths)

    received = []
    for k in range(4):
        pairs = []
        for t in range(2):
            for a in range(4):
                pairs.append((t * 4 + a, (a // 2) * 4 + (a + k + 2 * t) % 4))
        received.append(lax.ppermute(sent[k], ("tp", "x"), pairs))

    other_scale = send(scale, tp=1)
    both = joined(scale, other_scale)
    far = send(both, core=1)

    kv_cache, part = attend(
        received, queries, positions.reshape(128, 1), scale, other_scale, page_table
    )
    parts = lax.all_to_all(part, ("z", "tp"), 0, 0, tiled=True)
    result = merge(parts, queries, new_keys, new_values, scale, other_scale)
    whole = lax.all_to_all(result, ("yh", "z", "tp"), 0, 0, tiled=True)
    attended, scales = finish(whole, both, far)
    return (kv_cache, scales, attended)


def solution(mesh):
    names = tuple(SIZES)
    fine = Mesh(mesh.devices.reshape(tuple(SIZES.values())), names)
    seq, head = ("yh", "z"), ("x", "core")
    in_specs = (
        P(seq + head, None),
        P(seq, "tp"),
        P(),
        P(seq + ("tp",)),
        P(None, None, head),
        P(None, None, head),
        P(None, None, head),
        P(),
    )
    out_specs = (P(None, seq + ("tp",), None, head), P(), P(None, None, head))
    return jax.shard_map(body, mesh=fine, in_specs=in_specs, out_specs=out_specs, check_vma=False)
```

```python
import functools
import math

import jax
import jax.numpy as jnp
from jax import lax
from jax.experimental import pallas as pl
from jax.experimental.pallas import tpu as pltpu
from jax.sharding import Mesh, PartitionSpec as P

HD = 128
PAGE = 256
PIECE = 256
TILE = 320
GROUP = 8
MIB = 1024 * 1024
VMEM = 20 * MIB
SHARED = 16 * MIB

eps = 1e-05
clip_level = 2.5
masked_fill = -1e30
inverse = 1.0 / (float(HD) ** 0.5)

SIZES = {"yh": 2, "z": 8, "tp": 2, "x": 4, "core": 2}
ANYWHERE = pl.BlockSpec(memory_space=pl.ANY)
WHOLE = pl.BlockSpec(memory_space=pltpu.VMEM)
SCALAR = pl.BlockSpec(memory_space=pltpu.SMEM)


def params(limit):
    return pltpu.CompilerParams(vmem_limit_bytes=limit)


def cost(flops=0, size=0, exps=0):
    return pl.CostEstimate(flops=flops, bytes_accessed=size, transcendentals=exps)


def send(value, **steps):
    names = tuple(steps)
    sizes = [SIZES[name] for name in names]
    pairs = []
    for i in range(math.prod(sizes)):
        target, rest = 0, i
        place = []
        for n in reversed(sizes):
            place.insert(0, rest % n)
            rest //= n
        for at, n, name in zip(place, sizes, names):
            target = target * n + (at + steps[name]) % n
        pairs.append((i, target))
    return lax.ppermute(value, names if len(names) > 1 else names[0], pairs)


def in_vmem(values):
    return [pltpu.with_memory_space_constraint(value, pltpu.VMEM) for value in values]


def relay_kernel(count, picks, *refs):
    sources, outs, sems = refs[:count], refs[count + 1 + count : -1], refs[-1]
    copies = []
    for out, parts in zip(outs, picks):
        at = 0
        for i, start, rows in parts:
            copies.append(
                pltpu.make_async_copy(
                    sources[i].at[pl.ds(start, rows)], out.at[pl.ds(at, rows)], sems.at[len(copies)]
                )
            )
            at += rows
    for copy in copies:
        copy.start()
    for copy in copies:
        copy.wait()


def relay(values, after, picks=()):
    args = in_vmem(values)
    shapes = [jax.ShapeDtypeStruct(v.shape, v.dtype) for v in values]
    for parts in picks:
        shape = (sum(rows for _, _, rows in parts), values[0].shape[1])
        shapes.append(pltpu.VMEM(shape, values[0].dtype))
    return pl.pallas_call(
        functools.partial(relay_kernel, len(args), picks),
        in_specs=[ANYWHERE] * (len(args) + 1),
        out_specs=[ANYWHERE] * len(shapes),
        out_shape=shapes,
        input_output_aliases={i: i for i in range(len(args))},
        scratch_shapes=[
            pltpu.SemaphoreType.DMA((max(1, sum(len(p) for p in picks)),)),
        ],
        compiler_params=params(SHARED),
        cost_estimate=cost(),
    )(*args, after)


def keep_kernel(source, target, sem):
    copy = pltpu.make_async_copy(source, target, sem)
    copy.start()
    copy.wait()


def keep(value):
    return pl.pallas_call(
        keep_kernel,
        in_specs=[ANYWHERE],
        out_specs=ANYWHERE,
        out_shape=pltpu.VMEM(value.shape, value.dtype),
        scratch_shapes=[pltpu.SemaphoreType.DMA],
        compiler_params=params(SHARED),
        cost_estimate=cost(size=2 * value.size * value.dtype.itemsize),
    )(value)


def take_kernel(weight, out, sems):
    core, half = lax.axis_index("core"), lax.axis_index("x") % 2
    copies = []
    for i in range(4):
        copies.append(
            pltpu.make_async_copy(
                weight.at[
                    pl.ds(pl.multiple_of(half * PIECE, PIECE), PIECE),
                    pl.ds(pl.multiple_of((2 * i + core) * HD, HD), HD),
                ],
                out.at[:, pl.ds(i * HD, HD)],
                sems.at[i],
            )
        )
    for copy in copies:
        copy.start()
    for copy in copies:
        copy.wait()


def take(weight):
    return pl.pallas_call(
        take_kernel,
        in_specs=[ANYWHERE],
        out_specs=ANYWHERE,
        out_shape=pltpu.VMEM((PIECE, 4 * HD), weight.dtype),
        scratch_shapes=[pltpu.SemaphoreType.DMA((4,))],
        compiler_params=params(SHARED),
        cost_estimate=cost(size=MIB),
    )(weight)


def project_kernel(names, has_acc, last, own, sib, *refs):
    arrays = len(names)
    sources, refs = refs[:arrays], refs[arrays:]
    acc = lengths = None
    if has_acc:
        acc, refs = refs[0], refs[1:]
    if last:
        lengths, refs = refs[0], refs[1:]
    outs, (held, sems) = refs[:-2], refs[-2:]
    yh, z, x = lax.axis_index("yh"), lax.axis_index("z"), lax.axis_index("x")
    core = lax.axis_index("core")
    width = 4 * HD
    copies, columns, weights = [], [], []
    for source, pieces in zip(sources, names):
        if pieces is None:
            pieces = [(0, 0, None), (0, 0, None)]
            for j in range(4):
                lanes = pl.ds(pl.multiple_of((2 * j + core) * HD, HD), HD)
                copies.append(
                    pltpu.make_async_copy(
                        source.at[:, lanes], held.at[:, pl.ds(j * HD, HD)], sems.at[j]
                    )
                )
            source = held
        for j, (other, dz, mine) in enumerate(pieces):
            half = j if mine is None else (x + (0 if mine else 1)) % 2
            shard = ((yh + other) % 2) * 8 + (z + dz + 8) % 8
            columns.append(pl.multiple_of((shard * 2 + half) * PIECE, PIECE))
            weights.append((source, j * PIECE))
    for copy in copies:
        copy.start()
    for copy in copies:
        copy.wait()
    rows = own.shape[0]
    total = refs[-3] if last else outs[0]
    for piece, (column, (source, start)) in enumerate(zip(columns, weights)):
        weight = source[start : start + PIECE]
        for side, tokens in enumerate((own, sib)):
            for row in range(0, rows, TILE):
                value = jnp.dot(
                    tokens[pl.ds(row, TILE), pl.ds(column, PIECE)],
                    weight,
                    preferred_element_type=jnp.float32,
                )
                here = pl.ds(side * rows + row, TILE)
                if piece > 0:
                    total[here] += value
                elif has_acc:
                    total[here] = acc[here] + value
                else:
                    total[here] = value
    if not last:
        return
    squares = outs[1]
    part = jnp.zeros((1, width), jnp.float32)
    limit = jnp.where(yh == 0, lengths[0], lengths[1])
    for row in range(0, 2 * rows, TILE):
        value = total[row : row + TILE]
        goes = pl.multiple_of((row + core * rows) % (2 * rows), TILE)
        place = (z * 4 + x) * 2 * rows + goes + lax.broadcasted_iota(jnp.int32, value.shape, 0)
        kept = jnp.where(place < limit, value * value, 0.0)
        part = part + jnp.sum(kept, axis=0, keepdims=True)
        outs[0][pl.ds(goes, TILE)] = value
    squares[...] = jnp.broadcast_to(part[None], squares.shape)


def project(own, sib, pieces, acc=None, lengths=None):
    names = [ids for _, ids in pieces]
    n = sum(2 if ids is None else len(ids) for ids in names)
    rows, width = own.shape[0], 4 * HD
    last = lengths is not None
    in_specs = [WHOLE, WHOLE] + [ANYWHERE if ids is None else WHOLE for ids in names]
    args = [own, sib] + [value for value, _ in pieces]
    args = [
        value if spec is ANYWHERE else pltpu.with_memory_space_constraint(value, pltpu.VMEM)
        for value, spec in zip(args, in_specs)
    ]
    aliases = {}
    if acc is not None:
        in_specs.append(WHOLE)
        if not last:
            aliases = {len(args): 0}
        args.append(acc)
    scratch = [
        pltpu.VMEM((2 * PIECE, width), jnp.bfloat16),
        pltpu.SemaphoreType.DMA((4,)),
    ]
    if not last:
        out_shape = [pltpu.VMEM((2 * rows, width), jnp.float32)]
    else:
        in_specs.append(SCALAR)
        args.append(lengths)
        out_shape = [pltpu.VMEM((2 * rows, width), jnp.float32)]
        out_shape.append(jax.ShapeDtypeStruct((64, 1, width), jnp.float32))
        scratch.insert(0, pltpu.VMEM((2 * rows, width), jnp.float32))
    return pl.pallas_call(
        functools.partial(project_kernel, names, acc is not None, last),
        in_specs=in_specs,
        out_specs=[WHOLE] * len(out_shape),
        scratch_shapes=scratch,
        out_shape=out_shape,
        input_output_aliases=aliases,
        compiler_params=params(SHARED),
        cost_estimate=cost(4 * rows * PIECE * n * width, n * PIECE * width * 2),
    )(*args)


def quantize_kernel(proj, squares, lengths, *outs):
    x, tp = lax.axis_index("x"), lax.axis_index("tp")
    count = (lengths[0] + lengths[1]).astype(jnp.float32)
    scale = jnp.sqrt(jnp.sum(squares[:, 0, :], axis=0, keepdims=True) / count + eps)
    outs[4][...] = scale
    for k in range(4):
        head = pl.ds(pl.multiple_of(((x + k + 2 * tp) % 4) * HD, HD), HD)
        value = proj[:, head] * (1.0 / outs[4][:, head])
        outs[k][...] = jnp.clip(value, -clip_level, clip_level).astype(jnp.bfloat16)


def quantize(proj, squares, lengths):
    rows, width = proj.shape
    return pl.pallas_call(
        quantize_kernel,
        in_specs=[WHOLE, WHOLE, SCALAR],
        out_specs=[WHOLE] * 5,
        out_shape=[pltpu.VMEM((rows, HD), jnp.bfloat16)] * 4
        + [jax.ShapeDtypeStruct((1, width), jnp.float32)],
        compiler_params=params(VMEM),
        cost_estimate=cost(4 * rows * width, 6 * rows * width),
    )(pltpu.with_memory_space_constraint(proj, pltpu.VMEM), squares, lengths)


def head_scale(own, other, side):
    here = pl.ds(pl.multiple_of(lax.axis_index("x") * HD, HD), HD)
    return jnp.where(lax.axis_index("tp") == side, own[:, here], other[:, here])


def attend_kernel(
    pages, r0, r1, r2, r3, query, limits, own_scale, other_scale, cache, part, held, tops, totals, sems
):
    yh, z, x, tp = [lax.axis_index(name) for name in ("yh", "z", "x", "tp")]
    got = (r0, r1, r2, r3)
    rows = r0.shape[0]
    scales = [head_scale(own_scale, other_scale, side) for side in range(2)]
    first = (x - 2 * tp + 4) % 4
    for m in range(4):

        @pl.when(first == m)
        def _(m=m):
            for j in range(4):
                held[j // 2, pl.ds((j % 2) * rows, rows)] = got[(m - j) % 4][...]

    count = 2 * rows // PAGE
    copies = []
    for j in range(2):
        for b in range(count):
            copies.append(
                pltpu.make_async_copy(
                    held.at[j, pl.ds(b * PAGE, PAGE)], cache.at[j, pages[b]], sems.at[j, b]
                )
            )
    for copy in copies:
        copy.start()
    keys, values = held[0], held[1]
    seen = pl.multiple_of(yh * 32, 32)
    limit = jnp.concatenate([limits[pl.ds(s * 64 + seen, 32)] for s in range(2)], axis=0)
    limit = jnp.concatenate([limit, limit], axis=0)
    base = (z * 2 + tp) * 2 * rows
    for pair in range(GROUP // 2):
        asked = [
            query[s, pl.ds(seen, 32), g * HD : (g + 1) * HD]
            for g in (2 * pair, 2 * pair + 1)
            for s in range(2)
        ]
        asked = jnp.concatenate(asked, axis=0)
        scaled = (asked.astype(jnp.float32) * scales[0]).astype(jnp.bfloat16)
        score = (
            lax.dot_general(
                scaled, keys, (((1,), (1,)), ((), ())), preferred_element_type=jnp.float32
            )
            * inverse
        )
        mask = base + lax.broadcasted_iota(jnp.int32, score.shape, 1) < limit
        top = jnp.max(jnp.where(mask, score, masked_fill), axis=1, keepdims=True)
        weight = jnp.where(mask, jnp.exp(score - top), 0.0)
        total = jnp.sum(weight, axis=1, keepdims=True)
        summed = jnp.dot(weight.astype(jnp.bfloat16), values, preferred_element_type=jnp.float32)
        for side in range(2):
            g = 2 * pair + side
            for block in range(8):
                source = slice(side * 64 + block * 8, side * 64 + block * 8 + 8)
                target = 2 * block + g // 4, slice((g % 4) * 8, (g % 4) * 8 + 8)
                part[target] = summed[source]
                tops[target], totals[target] = [
                    jnp.broadcast_to(value[source], (8, HD)) for value in (top, total)
                ]
    here = lax.broadcasted_iota(jnp.int32, (32, HD), 0) == lax.broadcasted_iota(
        jnp.int32, (32, HD), 1
    )
    for share in range(16):
        for at, column in enumerate((tops, totals)):
            part[share, 32 + at : 33 + at] = jnp.sum(
                jnp.where(here, column[share], 0.0), axis=0, keepdims=True
            )
    for copy in copies:
        copy.wait()


def attend(received, query, limits, own_scale, other_scale, page_table):
    rows = received[0].shape[0]
    pages = 2 * rows // PAGE
    heads = 512
    return pl.pallas_call(
        attend_kernel,
        in_specs=[SCALAR] + [WHOLE] * 8,
        out_specs=[ANYWHERE, WHOLE],
        scratch_shapes=[
            pltpu.VMEM((2, 2 * rows, HD), jnp.bfloat16),
            pltpu.VMEM((16, 32, HD), jnp.float32),
            pltpu.VMEM((16, 32, HD), jnp.float32),
            pltpu.SemaphoreType.DMA((2, pages)),
        ],
        out_shape=[
            jax.ShapeDtypeStruct((2, pages, PAGE, HD), jnp.bfloat16),
            jax.ShapeDtypeStruct((16, 40, HD), jnp.float32),
        ],
        compiler_params=params(VMEM),
        cost_estimate=cost(8 * heads * rows * HD, 16 * rows * HD, 2 * heads * rows),
    )(page_table, *in_vmem(received), query, limits, own_scale, other_scale)


def merge_kernel(parts, query, new_key, new_value, own_scale, other_scale, out, rows):
    yh, z, tp = [lax.axis_index(name) for name in ("yh", "z", "tp")]
    seen = pl.multiple_of(yh * 32, 32)
    step, at = z // 4, pl.multiple_of((z % 4) * 8, 8)
    half = 4 * HD
    rows[:, :half] = query[step, pl.ds(seen, 32), pl.ds(pl.multiple_of(tp * half, half), half)].astype(
        jnp.float32
    )
    rows[:, half : half + HD] = new_key[step, pl.ds(seen, 32)].astype(jnp.float32)
    rows[:, half + HD :] = new_value[step, pl.ds(seen, 32)].astype(jnp.float32)
    key = rows[pl.ds(at, 8), half : half + HD]
    value = rows[pl.ds(at, 8), half + HD :]
    scale = head_scale(own_scale, other_scale, 1)
    own = [
        jnp.sum(rows[pl.ds(at, 8), g * HD : (g + 1) * HD] * key, axis=1, keepdims=True) * inverse
        for g in range(4)
    ]
    own = jnp.concatenate(own, axis=0)
    value = jnp.concatenate([value] * 4, axis=0)
    here = lax.broadcasted_iota(jnp.int32, (1, 32, HD), 1) == lax.broadcasted_iota(
        jnp.int32, (1, 32, HD), 2
    )
    top, total = [
        jnp.sum(jnp.where(here, parts[:, at : at + 1, :], 0.0), axis=2, keepdims=True)
        for at in (32, 33)
    ]
    overall = jnp.maximum(jnp.max(top, axis=0), own)
    factor = jnp.exp(top - overall[None])
    own_weight = jnp.exp(own - overall)
    denominator = jnp.sum(total * factor, axis=0) + own_weight
    summed = jnp.sum(parts[:, :32, :] * factor, axis=0)
    result = (summed * scale + own_weight * value) / denominator
    out[...] = jnp.broadcast_to(result.astype(out.dtype)[None], out.shape)


def merge(parts, query, new_key, new_value, own_scale, other_scale):
    return pl.pallas_call(
        merge_kernel,
        in_specs=[WHOLE] * 6,
        out_specs=WHOLE,
        out_shape=jax.ShapeDtypeStruct((32, 32, HD), jnp.bfloat16),
        scratch_shapes=[pltpu.VMEM((32, 6 * HD), jnp.float32)],
        compiler_params=params(VMEM),
        cost_estimate=cost(1 << 18, 1 << 19, 512),
    )(*in_vmem([parts]), query, new_key, new_value, own_scale, other_scale)


def finish_kernel(whole, both, far, attended, scales):
    for yh in range(2):
        for step in range(2):
            for side in range(2):
                blocks = [
                    whole[yh * 16 + 2 * (step * 4 + part) + side].astype(jnp.float32)
                    for part in range(4)
                ]
                for g in range(4):
                    value = jnp.concatenate([b[g * 8 : g * 8 + 8] for b in blocks], axis=0)
                    head = side * 4 + g
                    attended[step, yh * 32 : yh * 32 + 32, head * HD : (head + 1) * HD] = (
                        value.astype(attended.dtype)
                    )
    tp, core = lax.axis_index("tp"), lax.axis_index("core")
    for side in range(2):
        for i in range(4):
            lanes = slice(i * HD, (i + 1) * HD)
            for c in range(2):
                own = jnp.where(core == c, both[0:1, lanes], far[0:1, lanes])
                other = jnp.where(core == c, both[1:2, lanes], far[1:2, lanes])
                scales[side : side + 1, (2 * i + c) * HD : (2 * i + c + 1) * HD] = jnp.where(
                    tp == side, own, other
                )


def finish(whole, both, far):
    return pl.pallas_call(
        finish_kernel,
        in_specs=[WHOLE] * 3,
        out_specs=[WHOLE] * 2,
        out_shape=[
            jax.ShapeDtypeStruct((2, 64, GROUP * HD), jnp.bfloat16),
            jax.ShapeDtypeStruct((2, 8 * HD), jnp.float32),
        ],
        compiler_params=params(VMEM),
        cost_estimate=cost(0, MIB // 2),
    )(*in_vmem([whole]), both, far)


def body(tokens, kv_weight, lengths, page_table, queries, new_keys, new_values, positions):
    sibling = send(tokens, core=1)
    own = keep(pltpu.with_memory_space_constraint(tokens, pltpu.HBM))

    def swapped(ids):
        return [(other, dz, False) for other, dz, _ in ids]

    at = lambda dz: [(0, dz, True), (1, dz - (1 if dz > 0 else -1), True)]
    near, far = lambda dz: [(0, dz, True)], lambda dz: [(1, dz, True)]
    part = lambda i: (i, 0, PIECE)

    first = take(kv_weight)
    cross, up, down = send(first, yh=1), send(first, z=1), send(first, z=-1)
    cross, up, down, both_up, both_down = relay(
        [cross, up, down], own, [[part(1), part(0)], [part(2), part(0)]]
    )
    wave = [(kv_weight, None), (both_up, at(-1)), (down, near(1))]

    over, under = send(both_up, x=-1), send(down, x=1)
    up, down = send(both_up, z=1), send(both_down, z=-1)
    sib = keep(sibling)
    up, down, over, under = relay([up, down, over, under], sib)
    wave += [(over, swapped(at(-1))), (under, swapped(near(1))), (up, at(-2)), (down, at(2))]

    over, under = send(up, x=-1), send(down, x=1)
    next_up, next_down = send(up, z=1), send(down, z=-1)
    acc = project(own, sib, wave)[0]
    up, down, over, under, last = relay(
        [next_up, next_down, over, under], acc, [[(1, PIECE, PIECE)]]
    )
    wave = [(up, at(-3)), (down, at(3)), (over, swapped(at(-2))), (under, swapped(at(2)))]

    over, under = send(up, x=-1), send(down, x=1)
    next_up, next_down = send(up, z=1), send(last, z=-1)
    acc = project(own, sib, wave, acc)[0]
    up, down, over, under, last = relay([next_up, next_down, over, under], acc, [[part(0)]])
    wave = [(up, at(-4)), (down, far(3)), (over, swapped(at(-3))), (under, swapped(at(3)))]

    over, under = send(up, x=-1), send(down, x=1)
    cross, corner = send(last, yh=1), send(last, yh=1, x=1)
    acc = project(own, sib, wave, acc)[0]
    wave = [(over, swapped(at(-4))), (under, swapped(far(3)))]
    wave += [(cross, far(-4)), (corner, swapped(far(-4)))]
    proj, squares = project(own, sib, wave, acc, lengths)
    squares = lax.all_to_all(squares, ("yh", "z", "x"), 0, 0, tiled=True)
    *sent, scale = quantize(proj, squares, lengths)

    received = []
    for k in range(4):
        pairs = []
        for t in range(2):
            for a in range(4):
                pairs.append((t * 4 + a, (a // 2) * 4 + (a + k + 2 * t) % 4))
        received.append(lax.ppermute(sent[k], ("tp", "x"), pairs))

    other_scale = send(scale, tp=1)
    both = jnp.concatenate([scale, other_scale], axis=0)
    far = send(both, core=1)

    kv_cache, part = attend(
        received, queries, positions.reshape(128, 1), scale, other_scale, page_table
    )
    parts = lax.all_to_all(part, ("z", "tp"), 0, 0, tiled=True)
    result = merge(parts, queries, new_keys, new_values, scale, other_scale)
    whole = lax.all_to_all(result, ("yh", "z", "tp"), 0, 0, tiled=True)
    attended, scales = finish(whole, both, far)
    return (kv_cache, scales, attended)


def solution(mesh):
    names = tuple(SIZES)
    fine = Mesh(mesh.devices.reshape(tuple(SIZES.values())), names)
    seq, head = ("yh", "z"), ("x", "core")
    in_specs = (
        P(seq + head, None),
        P(seq, "tp"),
        P(),
        P(seq + ("tp",)),
        P(None, None, head),
        P(None, None, head),
        P(None, None, head),
        P(),
    )
    out_specs = (P(None, seq + ("tp",), None, head), P(), P(None, None, head))
    return jax.shard_map(body, mesh=fine, in_specs=in_specs, out_specs=out_specs, check_vma=False)
```

```python
import functools
import math

import jax
import jax.numpy as jnp
from jax import lax
from jax.experimental import pallas as pl
from jax.experimental.pallas import tpu as pltpu
from jax.sharding import Mesh, PartitionSpec as P

HD = 128
PAGE = 256
PIECE = 256
TILE = 320
GROUP = 8
MIB = 1024 * 1024
VMEM = 20 * MIB
SHARED = 16 * MIB

eps = 1e-05
clip_level = 2.5
masked_fill = -1e30
inverse = 1.0 / (float(HD) ** 0.5)
log2e = 1.4426950408889634

SIZES = {"yh": 2, "z": 8, "tp": 2, "x": 4, "core": 2}
ANYWHERE = pl.BlockSpec(memory_space=pl.ANY)
WHOLE = pl.BlockSpec(memory_space=pltpu.VMEM)
SCALAR = pl.BlockSpec(memory_space=pltpu.SMEM)


def params(limit):
    return pltpu.CompilerParams(vmem_limit_bytes=limit)


def cost(flops=0, size=0, exps=0):
    return pl.CostEstimate(flops=flops, bytes_accessed=size, transcendentals=exps)


def send(value, **steps):
    names = tuple(steps)
    sizes = [SIZES[name] for name in names]
    pairs = []
    for i in range(math.prod(sizes)):
        target, rest = 0, i
        place = []
        for n in reversed(sizes):
            place.insert(0, rest % n)
            rest //= n
        for at, n, name in zip(place, sizes, names):
            target = target * n + (at + steps[name]) % n
        pairs.append((i, target))
    return lax.ppermute(value, names if len(names) > 1 else names[0], pairs)


def in_vmem(values):
    return [pltpu.with_memory_space_constraint(value, pltpu.VMEM) for value in values]


def relay_kernel(count, picks, *refs):
    sources, outs, sems = refs[:count], refs[count + 1 + count : -1], refs[-1]
    copies = []
    for out, parts in zip(outs, picks):
        at = 0
        for i, start, rows in parts:
            copies.append(
                pltpu.make_async_copy(
                    sources[i].at[pl.ds(start, rows)], out.at[pl.ds(at, rows)], sems.at[len(copies)]
                )
            )
            at += rows
    for copy in copies:
        copy.start()
    for copy in copies:
        copy.wait()


def relay(values, after, picks=()):
    args = in_vmem(values)
    shapes = [jax.ShapeDtypeStruct(v.shape, v.dtype) for v in values]
    for parts in picks:
        shape = (sum(rows for _, _, rows in parts), values[0].shape[1])
        shapes.append(pltpu.VMEM(shape, values[0].dtype))
    return pl.pallas_call(
        functools.partial(relay_kernel, len(args), picks),
        in_specs=[ANYWHERE] * (len(args) + 1),
        out_specs=[ANYWHERE] * len(shapes),
        out_shape=shapes,
        input_output_aliases={i: i for i in range(len(args))},
        scratch_shapes=[
            pltpu.SemaphoreType.DMA((max(1, sum(len(p) for p in picks)),)),
        ],
        compiler_params=params(SHARED),
        cost_estimate=cost(),
    )(*args, after)


def picked_kernel(count, picks, *refs):
    relay_kernel(count, picks, *refs[:count], None, *[None] * count, *refs[count:])


def picked(values, picks):
    return pl.pallas_call(
        functools.partial(picked_kernel, len(values), picks),
        in_specs=[ANYWHERE] * len(values),
        out_specs=[ANYWHERE] * len(picks),
        out_shape=[
            pltpu.VMEM((sum(rows for _, _, rows in parts), values[0].shape[1]), values[0].dtype)
            for parts in picks
        ],
        scratch_shapes=[pltpu.SemaphoreType.DMA((sum(len(p) for p in picks),))],
        compiler_params=params(SHARED),
        cost_estimate=cost(),
    )(*in_vmem(values))


def keep_kernel(source, target, sem):
    copy = pltpu.make_async_copy(source, target, sem)
    copy.start()
    copy.wait()


def keep(value):
    return pl.pallas_call(
        keep_kernel,
        in_specs=[ANYWHERE],
        out_specs=ANYWHERE,
        out_shape=pltpu.VMEM(value.shape, value.dtype),
        scratch_shapes=[pltpu.SemaphoreType.DMA],
        compiler_params=params(SHARED),
        cost_estimate=cost(size=2 * value.size * value.dtype.itemsize),
    )(value)


def take_kernel(weight, out, sems):
    core, half = lax.axis_index("core"), lax.axis_index("x") % 2
    copies = []
    for i in range(4):
        copies.append(
            pltpu.make_async_copy(
                weight.at[
                    pl.ds(pl.multiple_of(half * PIECE, PIECE), PIECE),
                    pl.ds(pl.multiple_of((2 * i + core) * HD, HD), HD),
                ],
                out.at[:, pl.ds(i * HD, HD)],
                sems.at[i],
            )
        )
    for copy in copies:
        copy.start()
    for copy in copies:
        copy.wait()


def take(weight):
    return pl.pallas_call(
        take_kernel,
        in_specs=[ANYWHERE],
        out_specs=ANYWHERE,
        out_shape=pltpu.VMEM((PIECE, 4 * HD), weight.dtype),
        scratch_shapes=[pltpu.SemaphoreType.DMA((4,))],
        compiler_params=params(SHARED),
        cost_estimate=cost(size=MIB),
    )(weight)


def project_kernel(names, has_acc, last, own, sib, *refs):
    arrays = len(names)
    sources, refs = refs[:arrays], refs[arrays:]
    acc = lengths = None
    if has_acc:
        acc, refs = refs[0], refs[1:]
    if last:
        lengths, refs = refs[0], refs[1:]
    outs, (held, sems) = refs[:-2], refs[-2:]
    yh, z, x = lax.axis_index("yh"), lax.axis_index("z"), lax.axis_index("x")
    core = lax.axis_index("core")
    width = 4 * HD
    copies, columns, weights = [], [], []
    for source, pieces in zip(sources, names):
        if pieces is None:
            pieces = [(0, 0, None), (0, 0, None)]
            for j in range(4):
                lanes = pl.ds(pl.multiple_of((2 * j + core) * HD, HD), HD)
                copies.append(
                    pltpu.make_async_copy(
                        source.at[:, lanes], held.at[:, pl.ds(j * HD, HD)], sems.at[j]
                    )
                )
            source = held
        for j, (other, dz, mine) in enumerate(pieces):
            half = j if mine is None else (x + (0 if mine else 1)) % 2
            shard = ((yh + other) % 2) * 8 + (z + dz + 8) % 8
            columns.append(pl.multiple_of((shard * 2 + half) * PIECE, PIECE))
            weights.append((source, j * PIECE))
    for copy in copies:
        copy.start()
    for copy in copies:
        copy.wait()
    rows = own.shape[0]
    total = refs[-3] if last else outs[0]
    for piece, (column, (source, start)) in enumerate(zip(columns, weights)):
        weight = source[start : start + PIECE]
        for side, tokens in enumerate((own, sib)):
            for row in range(0, rows, TILE):
                value = jnp.dot(
                    tokens[pl.ds(row, TILE), pl.ds(column, PIECE)],
                    weight,
                    preferred_element_type=jnp.float32,
                )
                here = pl.ds(side * rows + row, TILE)
                if piece > 0:
                    total[here] += value
                elif has_acc:
                    total[here] = acc[here] + value
                else:
                    total[here] = value
    if not last:
        return
    squares = outs[1]
    part = jnp.zeros((1, width), jnp.float32)
    limit = jnp.where(yh == 0, lengths[0], lengths[1])
    for row in range(0, 2 * rows, TILE):
        value = total[row : row + TILE]
        goes = pl.multiple_of((row + core * rows) % (2 * rows), TILE)
        place = (z * 4 + x) * 2 * rows + goes + lax.broadcasted_iota(jnp.int32, value.shape, 0)
        kept = jnp.where(place < limit, value * value, 0.0)
        part = part + jnp.sum(kept, axis=0, keepdims=True)
        outs[0][pl.ds(goes, TILE)] = value
    for i in range(4):
        lanes = part[None, :, i * HD : (i + 1) * HD]
        squares[:, i : i + 1, :] = jnp.broadcast_to(lanes, (squares.shape[0], 1, HD))


def project(own, sib, pieces, acc=None, lengths=None):
    names = [ids for _, ids in pieces]
    n = sum(2 if ids is None else len(ids) for ids in names)
    rows, width = own.shape[0], 4 * HD
    last = lengths is not None
    in_specs = [WHOLE, WHOLE] + [ANYWHERE if ids is None else WHOLE for ids in names]
    args = [own, sib] + [value for value, _ in pieces]
    args = [
        value if spec is ANYWHERE else pltpu.with_memory_space_constraint(value, pltpu.VMEM)
        for value, spec in zip(args, in_specs)
    ]
    aliases = {}
    if acc is not None:
        in_specs.append(WHOLE)
        if not last:
            aliases = {len(args): 0}
        args.append(acc)
    scratch = [
        pltpu.VMEM((2 * PIECE, width), jnp.bfloat16),
        pltpu.SemaphoreType.DMA((4,)),
    ]
    if not last:
        out_shape = [pltpu.VMEM((2 * rows, width), jnp.float32)]
    else:
        in_specs.append(SCALAR)
        args.append(lengths)
        out_shape = [pltpu.VMEM((2 * rows, width), jnp.float32)]
        out_shape.append(jax.ShapeDtypeStruct((64, 4, HD), jnp.float32))
        scratch.insert(0, pltpu.VMEM((2 * rows, width), jnp.float32))
    return pl.pallas_call(
        functools.partial(project_kernel, names, acc is not None, last),
        in_specs=in_specs,
        out_specs=[WHOLE] * len(out_shape),
        scratch_shapes=scratch,
        out_shape=out_shape,
        input_output_aliases=aliases,
        compiler_params=params(SHARED),
        cost_estimate=cost(4 * rows * PIECE * n * width, n * PIECE * width * 2),
    )(*args)


def quantize_kernel(proj, squares, lengths, *outs):
    x, tp = lax.axis_index("x"), lax.axis_index("tp")
    count = (lengths[0] + lengths[1]).astype(jnp.float32)
    mean = jnp.sum(squares[...], axis=0) / count
    for i in range(4):
        outs[4][:, i * HD : (i + 1) * HD] = jnp.sqrt(mean[i : i + 1] + eps)
    for k in range(4):
        head = pl.ds(pl.multiple_of(((x + k + 2 * tp) % 4) * HD, HD), HD)
        value = proj[:, head] * (1.0 / outs[4][:, head])
        outs[k][...] = jnp.clip(value, -clip_level, clip_level).astype(jnp.bfloat16)


def quantize(proj, squares, lengths):
    rows, width = proj.shape
    return pl.pallas_call(
        quantize_kernel,
        in_specs=[WHOLE, WHOLE, SCALAR],
        out_specs=[WHOLE] * 5,
        out_shape=[pltpu.VMEM((rows, HD), jnp.bfloat16)] * 4
        + [jax.ShapeDtypeStruct((1, width), jnp.float32)],
        compiler_params=params(VMEM),
        cost_estimate=cost(4 * rows * width, 6 * rows * width),
    )(pltpu.with_memory_space_constraint(proj, pltpu.VMEM), squares, lengths)


def head_scale(own, other, side):
    here = pl.ds(pl.multiple_of(lax.axis_index("x") * HD, HD), HD)
    return jnp.where(lax.axis_index("tp") == side, own[:, here], other[:, here])


def attend_kernel(
    pages, r0, r1, r2, r3, query, limits, own_scale, other_scale, cache, part, held, tops, totals, sems
):
    yh, z, x, tp = [lax.axis_index(name) for name in ("yh", "z", "x", "tp")]
    got = (r0, r1, r2, r3)
    rows = r0.shape[0]
    scales = [head_scale(own_scale, other_scale, side) for side in range(2)]
    first = (x - 2 * tp + 4) % 4
    for m in range(4):

        @pl.when(first == m)
        def _(m=m):
            for j in range(4):
                held[j // 2, pl.ds((j % 2) * rows, rows)] = got[(m - j) % 4][...]

    count = 2 * rows // PAGE
    copies = []
    for j in range(2):
        for b in range(count):
            copies.append(
                pltpu.make_async_copy(
                    held.at[j, pl.ds(b * PAGE, PAGE)], cache.at[j, pages[b]], sems.at[j, b]
                )
            )
    for copy in copies:
        copy.start()
    keys, values = held[0], held[1]
    seen = pl.multiple_of(yh * 32, 32)
    limit = jnp.concatenate([limits[pl.ds(s * 64 + seen, 32)] for s in range(2)], axis=0)
    limit = jnp.concatenate([limit, limit], axis=0)
    place = (z * 2 + tp) * 2 * rows + lax.broadcasted_iota(jnp.int32, (1, 2 * rows), 1)
    for pair in range(GROUP // 2):
        asked = [
            query[s, pl.ds(seen, 32), g * HD : (g + 1) * HD]
            for g in (2 * pair, 2 * pair + 1)
            for s in range(2)
        ]
        asked = jnp.concatenate(asked, axis=0)
        scaled = (asked.astype(jnp.float32) * scales[0]).astype(jnp.bfloat16)
        score = lax.dot_general(
            scaled, keys, (((1,), (1,)), ((), ())), preferred_element_type=jnp.float32
        )
        score = jnp.where(place < limit, score, masked_fill)
        top = jnp.max(score, axis=1, keepdims=True)
        weight = jnp.exp2((score - top) * (inverse * log2e))
        top = top * inverse
        total = jnp.sum(weight, axis=1, keepdims=True)
        summed = jnp.dot(weight.astype(jnp.bfloat16), values, preferred_element_type=jnp.float32)
        for side in range(2):
            g = 2 * pair + side
            for block in range(8):
                source = slice(side * 64 + block * 8, side * 64 + block * 8 + 8)
                target = 2 * block + g // 4, slice((g % 4) * 8, (g % 4) * 8 + 8)
                part[target] = summed[source]
                tops[target], totals[target] = [
                    jnp.broadcast_to(value[source], (8, HD)) for value in (top, total)
                ]
    here = lax.broadcasted_iota(jnp.int32, (32, HD), 0) == lax.broadcasted_iota(
        jnp.int32, (32, HD), 1
    )
    for share in range(16):
        for at, column in enumerate((tops, totals)):
            part[share, 32 + at : 33 + at] = jnp.sum(
                jnp.where(here, column[share], 0.0), axis=0, keepdims=True
            )
    for copy in copies:
        copy.wait()


def attend(received, query, limits, own_scale, other_scale, page_table):
    rows = received[0].shape[0]
    pages = 2 * rows // PAGE
    heads = 512
    return pl.pallas_call(
        attend_kernel,
        in_specs=[SCALAR] + [WHOLE] * 8,
        out_specs=[ANYWHERE, WHOLE],
        scratch_shapes=[
            pltpu.VMEM((2, 2 * rows, HD), jnp.bfloat16),
            pltpu.VMEM((16, 32, HD), jnp.float32),
            pltpu.VMEM((16, 32, HD), jnp.float32),
            pltpu.SemaphoreType.DMA((2, pages)),
        ],
        out_shape=[
            jax.ShapeDtypeStruct((2, pages, PAGE, HD), jnp.bfloat16),
            jax.ShapeDtypeStruct((16, 40, HD), jnp.float32),
        ],
        compiler_params=params(VMEM),
        cost_estimate=cost(8 * heads * rows * HD, 16 * rows * HD, 2 * heads * rows),
    )(page_table, *in_vmem(received), query, limits, own_scale, other_scale)


def merge_kernel(parts, query, new_key, new_value, own_scale, other_scale, out, rows):
    yh, z, tp = [lax.axis_index(name) for name in ("yh", "z", "tp")]
    seen = pl.multiple_of(yh * 32, 32)
    step, at = z // 4, pl.multiple_of((z % 4) * 8, 8)
    half = 4 * HD
    rows[:, :half] = query[step, pl.ds(seen, 32), pl.ds(pl.multiple_of(tp * half, half), half)].astype(
        jnp.float32
    )
    rows[:, half : half + HD] = new_key[step, pl.ds(seen, 32)].astype(jnp.float32)
    rows[:, half + HD :] = new_value[step, pl.ds(seen, 32)].astype(jnp.float32)
    key = rows[pl.ds(at, 8), half : half + HD]
    value = rows[pl.ds(at, 8), half + HD :]
    scale = head_scale(own_scale, other_scale, 1)
    own = [
        jnp.sum(rows[pl.ds(at, 8), g * HD : (g + 1) * HD] * key, axis=1, keepdims=True) * inverse
        for g in range(4)
    ]
    own = jnp.concatenate(own, axis=0)
    value = jnp.concatenate([value] * 4, axis=0)
    here = lax.broadcasted_iota(jnp.int32, (1, 32, HD), 1) == lax.broadcasted_iota(
        jnp.int32, (1, 32, HD), 2
    )
    top, total = [
        jnp.sum(jnp.where(here, parts[:, at : at + 1, :], 0.0), axis=2, keepdims=True)
        for at in (32, 33)
    ]
    overall = jnp.maximum(jnp.max(top, axis=0), own)
    factor = jnp.exp(top - overall[None])
    own_weight = jnp.exp(own - overall)
    denominator = jnp.sum(total * factor, axis=0) + own_weight
    summed = jnp.sum(parts[:, :32, :] * factor, axis=0)
    result = (summed * scale + own_weight * value) / denominator
    out[...] = jnp.broadcast_to(result.astype(out.dtype)[None], out.shape)


def merge(parts, query, new_key, new_value, own_scale, other_scale):
    return pl.pallas_call(
        merge_kernel,
        in_specs=[WHOLE] * 6,
        out_specs=WHOLE,
        out_shape=jax.ShapeDtypeStruct((32, 32, HD), jnp.bfloat16),
        scratch_shapes=[pltpu.VMEM((32, 6 * HD), jnp.float32)],
        compiler_params=params(VMEM),
        cost_estimate=cost(1 << 18, 1 << 19, 512),
    )(*in_vmem([parts]), query, new_key, new_value, own_scale, other_scale)


def finish_kernel(whole, both, far, attended, scales):
    for yh in range(2):
        for step in range(2):
            for side in range(2):
                blocks = [
                    whole[yh * 16 + 2 * (step * 4 + part) + side].astype(jnp.float32)
                    for part in range(4)
                ]
                for g in range(4):
                    value = jnp.concatenate([b[g * 8 : g * 8 + 8] for b in blocks], axis=0)
                    head = side * 4 + g
                    attended[step, yh * 32 : yh * 32 + 32, head * HD : (head + 1) * HD] = (
                        value.astype(attended.dtype)
                    )
    tp, core = lax.axis_index("tp"), lax.axis_index("core")
    for side in range(2):
        for i in range(4):
            lanes = slice(i * HD, (i + 1) * HD)
            for c in range(2):
                own = jnp.where(core == c, both[0:1, lanes], far[0:1, lanes])
                other = jnp.where(core == c, both[1:2, lanes], far[1:2, lanes])
                scales[side : side + 1, (2 * i + c) * HD : (2 * i + c + 1) * HD] = jnp.where(
                    tp == side, own, other
                )


def finish(whole, both, far):
    return pl.pallas_call(
        finish_kernel,
        in_specs=[WHOLE] * 3,
        out_specs=[WHOLE] * 2,
        out_shape=[
            jax.ShapeDtypeStruct((2, 64, GROUP * HD), jnp.bfloat16),
            jax.ShapeDtypeStruct((2, 8 * HD), jnp.float32),
        ],
        compiler_params=params(VMEM),
        cost_estimate=cost(0, MIB // 2),
    )(*in_vmem([whole]), both, far)


def body(tokens, kv_weight, lengths, page_table, queries, new_keys, new_values, positions):
    sibling = send(tokens, core=1)
    own = keep(pltpu.with_memory_space_constraint(tokens, pltpu.HBM))

    def swapped(ids):
        return [(other, dz, False) for other, dz, _ in ids]

    at = lambda dz: [(0, dz, True), (1, dz - (1 if dz > 0 else -1), True)]
    near, far = lambda dz: [(0, dz, True)], lambda dz: [(1, dz, True)]
    part = lambda i: (i, 0, PIECE)

    first = take(kv_weight)
    cross, up, down = send(first, yh=1), send(first, z=1), send(first, z=-1)
    cross, up, down, both_up, both_down = relay(
        [cross, up, down], own, [[part(1), part(0)], [part(2), part(0)]]
    )
    wave = [(kv_weight, None), (both_up, at(-1)), (down, near(1))]

    over, under = send(both_up, x=-1), send(down, x=1)
    next_up, next_down = send(both_up, z=1), send(both_down, z=-1)
    sib = keep(sibling)
    up, down, last = relay([next_up, next_down], sib, [[part(0)]])
    wave += [(over, swapped(at(-1))), (under, swapped(near(1))), (up, at(-2)), (down, at(2))]
    (over,) = picked([over], [[part(0)]])

    side, over, under = send(over, yh=1), send(last, x=-1), send(down, x=1)
    next_up, next_down = send(up, z=1), send(down, z=-1)
    acc = project(own, sib, wave)[0]
    up, down, last, next_last = relay(
        [next_up, next_down], acc, [[part(0)], [(1, PIECE, PIECE)]]
    )
    wave = [(up, at(-3)), (down, at(3)), (over, swapped(near(-2))), (under, swapped(at(2)))]
    wave += [(side, swapped(far(-1)))]

    side, over, under = send(over, yh=1), send(last, x=-1), send(down, x=1)
    next_up, next_down = send(up, z=1), send(next_last, z=-1)
    acc = project(own, sib, wave, acc)[0]
    up, down, last, next_last = relay(
        [next_up, next_down], acc, [[part(0)], [(0, PIECE, PIECE)]]
    )
    wave = [(up, at(-4)), (down, far(3)), (over, swapped(near(-3))), (under, swapped(at(3)))]
    wave += [(side, swapped(far(-2)))]

    side, under, cross = send(over, yh=1), send(down, x=1), send(next_last, z=1)
    corner, over = send(last, yh=1, x=-1), send(last, x=-1)
    acc = project(own, sib, wave, acc)[0]
    wave = [(over, swapped(near(-4))), (under, swapped(far(3))), (side, swapped(far(-3)))]
    wave += [(cross, far(-4)), (corner, swapped(far(-4)))]
    proj, squares = project(own, sib, wave, acc, lengths)
    squares = lax.all_to_all(squares, ("x", "z", "yh"), 0, 0, tiled=True)
    *sent, scale = quantize(proj, squares, lengths)

    received = []
    for k in range(4):
        pairs = []
        for t in range(2):
            for a in range(4):
                pairs.append((t * 4 + a, (a // 2) * 4 + (a + k + 2 * t) % 4))
        received.append(lax.ppermute(sent[k], ("tp", "x"), pairs))

    other_scale = send(scale, tp=1)
    both = jnp.concatenate([scale, other_scale], axis=0)
    far = send(both, core=1)

    kv_cache, part = attend(
        received, queries, positions.reshape(128, 1), scale, other_scale, page_table
    )
    parts = lax.all_to_all(part, ("z", "tp"), 0, 0, tiled=True)
    result = merge(parts, queries, new_keys, new_values, scale, other_scale)
    whole = lax.all_to_all(result, ("yh", "z", "tp"), 0, 0, tiled=True)
    attended, scales = finish(whole, both, far)
    return (kv_cache, scales, attended)


def solution(mesh):
    names = tuple(SIZES)
    fine = Mesh(mesh.devices.reshape(tuple(SIZES.values())), names)
    seq, head = ("yh", "z"), ("x", "core")
    in_specs = (
        P(seq + head, None),
        P(seq, "tp"),
        P(),
        P(seq + ("tp",)),
        P(None, None, head),
        P(None, None, head),
        P(None, None, head),
        P(),
    )
    out_specs = (P(None, seq + ("tp",), None, head), P(), P(None, None, head))
    return jax.shard_map(body, mesh=fine, in_specs=in_specs, out_specs=out_specs, check_vma=False)
```

```python
import functools
import math

import jax
import jax.numpy as jnp
from jax import lax
from jax.experimental import pallas as pl
from jax.experimental.pallas import tpu as pltpu
from jax.sharding import Mesh, PartitionSpec as P

HD = 128
PAGE = 256
PIECE = 256
TILE = 320
GROUP = 8
MIB = 1024 * 1024
VMEM = 20 * MIB
SHARED = 16 * MIB

eps = 1e-05
clip_level = 2.5
masked_fill = -1e30
inverse = 1.0 / (float(HD) ** 0.5)
log2e = 1.4426950408889634

SIZES = {"yh": 2, "z": 8, "tp": 2, "x": 4, "core": 2}
ANYWHERE = pl.BlockSpec(memory_space=pl.ANY)
WHOLE = pl.BlockSpec(memory_space=pltpu.VMEM)
SCALAR = pl.BlockSpec(memory_space=pltpu.SMEM)


def params(limit):
    return pltpu.CompilerParams(vmem_limit_bytes=limit)


def cost(flops=0, size=0, exps=0):
    return pl.CostEstimate(flops=flops, bytes_accessed=size, transcendentals=exps)


def send(value, **steps):
    names = tuple(steps)
    sizes = [SIZES[name] for name in names]
    pairs = []
    for i in range(math.prod(sizes)):
        target, rest = 0, i
        place = []
        for n in reversed(sizes):
            place.insert(0, rest % n)
            rest //= n
        for at, n, name in zip(place, sizes, names):
            target = target * n + (at + steps[name]) % n
        pairs.append((i, target))
    return lax.ppermute(value, names if len(names) > 1 else names[0], pairs)


def in_vmem(values):
    return [pltpu.with_memory_space_constraint(value, pltpu.VMEM) for value in values]


def relay_kernel(count, picks, *refs):
    sources, outs, sems = refs[:count], refs[count + 1 + count : -1], refs[-1]
    copies = []
    for out, parts in zip(outs, picks):
        at = 0
        for i, start, rows in parts:
            copies.append(
                pltpu.make_async_copy(
                    sources[i].at[pl.ds(start, rows)], out.at[pl.ds(at, rows)], sems.at[len(copies)]
                )
            )
            at += rows
    for copy in copies:
        copy.start()
    for copy in copies:
        copy.wait()


def relay(values, after, picks=()):
    args = in_vmem(values)
    shapes = [jax.ShapeDtypeStruct(v.shape, v.dtype) for v in values]
    for parts in picks:
        shape = (sum(rows for _, _, rows in parts), values[0].shape[1])
        shapes.append(pltpu.VMEM(shape, values[0].dtype))
    return pl.pallas_call(
        functools.partial(relay_kernel, len(args), picks),
        in_specs=[ANYWHERE] * (len(args) + 1),
        out_specs=[ANYWHERE] * len(shapes),
        out_shape=shapes,
        input_output_aliases={i: i for i in range(len(args))},
        scratch_shapes=[
            pltpu.SemaphoreType.DMA((max(1, sum(len(p) for p in picks)),)),
        ],
        compiler_params=params(SHARED),
        cost_estimate=cost(),
    )(*args, after)


def picked_kernel(count, picks, *refs):
    relay_kernel(count, picks, *refs[:count], None, *[None] * count, *refs[count:])


def picked(values, picks):
    return pl.pallas_call(
        functools.partial(picked_kernel, len(values), picks),
        in_specs=[ANYWHERE] * len(values),
        out_specs=[ANYWHERE] * len(picks),
        out_shape=[
            pltpu.VMEM((sum(rows for _, _, rows in parts), values[0].shape[1]), values[0].dtype)
            for parts in picks
        ],
        scratch_shapes=[pltpu.SemaphoreType.DMA((sum(len(p) for p in picks),))],
        compiler_params=params(SHARED),
        cost_estimate=cost(),
    )(*in_vmem(values))


def keep_kernel(source, target, sem):
    copy = pltpu.make_async_copy(source, target, sem)
    copy.start()
    copy.wait()


def keep(value):
    return pl.pallas_call(
        keep_kernel,
        in_specs=[ANYWHERE],
        out_specs=ANYWHERE,
        out_shape=pltpu.VMEM(value.shape, value.dtype),
        scratch_shapes=[pltpu.SemaphoreType.DMA],
        compiler_params=params(SHARED),
        cost_estimate=cost(size=2 * value.size * value.dtype.itemsize),
    )(value)


def take_kernel(weight, out, sems):
    core, half = lax.axis_index("core"), lax.axis_index("x") % 2
    copies = []
    for i in range(4):
        copies.append(
            pltpu.make_async_copy(
                weight.at[
                    pl.ds(pl.multiple_of(half * PIECE, PIECE), PIECE),
                    pl.ds(pl.multiple_of((2 * i + core) * HD, HD), HD),
                ],
                out.at[:, pl.ds(i * HD, HD)],
                sems.at[i],
            )
        )
    for copy in copies:
        copy.start()
    for copy in copies:
        copy.wait()


def take(weight):
    return pl.pallas_call(
        take_kernel,
        in_specs=[ANYWHERE],
        out_specs=ANYWHERE,
        out_shape=pltpu.VMEM((PIECE, 4 * HD), weight.dtype),
        scratch_shapes=[pltpu.SemaphoreType.DMA((4,))],
        compiler_params=params(SHARED),
        cost_estimate=cost(size=MIB),
    )(weight)


def project_kernel(names, has_acc, last, own, sib, *refs):
    arrays = len(names)
    sources, refs = refs[:arrays], refs[arrays:]
    acc = lengths = None
    if has_acc:
        acc, refs = refs[0], refs[1:]
    if last:
        lengths, refs = refs[0], refs[1:]
    outs, (held, sems) = refs[:-2], refs[-2:]
    yh, z, x = lax.axis_index("yh"), lax.axis_index("z"), lax.axis_index("x")
    core = lax.axis_index("core")
    width = 4 * HD
    copies, columns, weights = [], [], []
    for source, pieces in zip(sources, names):
        if pieces is None:
            pieces = [(0, 0, None), (0, 0, None)]
            for j in range(4):
                lanes = pl.ds(pl.multiple_of((2 * j + core) * HD, HD), HD)
                copies.append(
                    pltpu.make_async_copy(
                        source.at[:, lanes], held.at[:, pl.ds(j * HD, HD)], sems.at[j]
                    )
                )
            source = held
        for j, (other, dz, mine) in enumerate(pieces):
            half = j if mine is None else (x + (0 if mine else 1)) % 2
            shard = ((yh + other) % 2) * 8 + (z + dz + 8) % 8
            columns.append(pl.multiple_of((shard * 2 + half) * PIECE, PIECE))
            weights.append((source, j * PIECE))
    for copy in copies:
        copy.start()
    for copy in copies:
        copy.wait()
    rows = own.shape[0]
    total = refs[-3] if last else outs[0]
    for piece, (column, (source, start)) in enumerate(zip(columns, weights)):
        weight = source[start : start + PIECE]
        for side, tokens in enumerate((own, sib)):
            for row in range(0, rows, TILE):
                value = jnp.dot(
                    tokens[pl.ds(row, TILE), pl.ds(column, PIECE)],
                    weight,
                    preferred_element_type=jnp.float32,
                )
                here = pl.ds(side * rows + row, TILE)
                if piece > 0:
                    total[here] += value
                elif has_acc:
                    total[here] = acc[here] + value
                else:
                    total[here] = value
    if not last:
        return
    squares = outs[1]
    part = jnp.zeros((1, width), jnp.float32)
    limit = jnp.where(yh == 0, lengths[0], lengths[1])
    for row in range(0, 2 * rows, TILE):
        value = total[row : row + TILE]
        goes = pl.multiple_of((row + core * rows) % (2 * rows), TILE)
        place = (z * 4 + x) * 2 * rows + goes + lax.broadcasted_iota(jnp.int32, value.shape, 0)
        kept = jnp.where(place < limit, value * value, 0.0)
        part = part + jnp.sum(kept, axis=0, keepdims=True)
        outs[0][pl.ds(goes, TILE)] = value
    for i in range(4):
        lanes = part[None, :, i * HD : (i + 1) * HD]
        squares[:, i : i + 1, :] = jnp.broadcast_to(lanes, (squares.shape[0], 1, HD))


def project(own, sib, pieces, acc=None, lengths=None):
    names = [ids for _, ids in pieces]
    n = sum(2 if ids is None else len(ids) for ids in names)
    rows, width = own.shape[0], 4 * HD
    last = lengths is not None
    in_specs = [WHOLE, WHOLE] + [ANYWHERE if ids is None else WHOLE for ids in names]
    args = [own, sib] + [value for value, _ in pieces]
    args = [
        value if spec is ANYWHERE else pltpu.with_memory_space_constraint(value, pltpu.VMEM)
        for value, spec in zip(args, in_specs)
    ]
    aliases = {}
    if acc is not None:
        in_specs.append(WHOLE)
        if not last:
            aliases = {len(args): 0}
        args.append(acc)
    scratch = [
        pltpu.VMEM((2 * PIECE, width), jnp.bfloat16),
        pltpu.SemaphoreType.DMA((4,)),
    ]
    if not last:
        out_shape = [pltpu.VMEM((2 * rows, width), jnp.float32)]
    else:
        in_specs.append(SCALAR)
        args.append(lengths)
        out_shape = [pltpu.VMEM((2 * rows, width), jnp.float32)]
        out_shape.append(jax.ShapeDtypeStruct((64, 4, HD), jnp.float32))
        scratch.insert(0, pltpu.VMEM((2 * rows, width), jnp.float32))
    return pl.pallas_call(
        functools.partial(project_kernel, names, acc is not None, last),
        in_specs=in_specs,
        out_specs=[WHOLE] * len(out_shape),
        scratch_shapes=scratch,
        out_shape=out_shape,
        input_output_aliases=aliases,
        compiler_params=params(SHARED),
        cost_estimate=cost(4 * rows * PIECE * n * width, n * PIECE * width * 2),
    )(*args)


def quantize_kernel(proj, squares, lengths, *outs):
    x, tp = lax.axis_index("x"), lax.axis_index("tp")
    count = (lengths[0] + lengths[1]).astype(jnp.float32)
    mean = jnp.sum(squares[...], axis=0) / count
    for i in range(4):
        outs[4][:, i * HD : (i + 1) * HD] = jnp.sqrt(mean[i : i + 1] + eps)
    for k in range(4):
        head = pl.ds(pl.multiple_of(((x + k + 2 * tp) % 4) * HD, HD), HD)
        value = proj[:, head] * (1.0 / outs[4][:, head])
        outs[k][...] = jnp.clip(value, -clip_level, clip_level).astype(jnp.bfloat16)


def quantize(proj, squares, lengths):
    rows, width = proj.shape
    return pl.pallas_call(
        quantize_kernel,
        in_specs=[WHOLE, WHOLE, SCALAR],
        out_specs=[WHOLE] * 5,
        out_shape=[pltpu.VMEM((rows, HD), jnp.bfloat16)] * 4
        + [jax.ShapeDtypeStruct((1, width), jnp.float32)],
        compiler_params=params(VMEM),
        cost_estimate=cost(4 * rows * width, 6 * rows * width),
    )(pltpu.with_memory_space_constraint(proj, pltpu.VMEM), squares, lengths)


def head_scale(own, other, side):
    here = pl.ds(pl.multiple_of(lax.axis_index("x") * HD, HD), HD)
    return jnp.where(lax.axis_index("tp") == side, own[:, here], other[:, here])


def attend_kernel(
    pages, r0, r1, r2, r3, query, limits, own_scale, other_scale, cache, part, held, tops, totals, sems
):
    yh, z, x, tp = [lax.axis_index(name) for name in ("yh", "z", "x", "tp")]
    got = (r0, r1, r2, r3)
    rows = r0.shape[0]
    scales = [head_scale(own_scale, other_scale, side) for side in range(2)]
    first = (x - 2 * tp + 4) % 4
    for m in range(4):

        @pl.when(first == m)
        def _(m=m):
            for j in range(4):
                held[j // 2, pl.ds((j % 2) * rows, rows)] = got[(m - j) % 4][...]

    count = 2 * rows // PAGE
    copies = []
    for j in range(2):
        for b in range(count):
            copies.append(
                pltpu.make_async_copy(
                    held.at[j, pl.ds(b * PAGE, PAGE)], cache.at[j, pages[b]], sems.at[j, b]
                )
            )
    for copy in copies:
        copy.start()
    keys, values = held[0], held[1]
    seen = pl.multiple_of(yh * 32, 32)
    limit = jnp.concatenate([limits[pl.ds(s * 64 + seen, 32)] for s in range(2)], axis=0)
    limit = jnp.concatenate([limit, limit], axis=0)
    place = (z * 2 + tp) * 2 * rows + lax.broadcasted_iota(jnp.int32, (1, 2 * rows), 1)
    for pair in range(GROUP // 2):
        asked = [
            query[s, pl.ds(seen, 32), g * HD : (g + 1) * HD]
            for g in (2 * pair, 2 * pair + 1)
            for s in range(2)
        ]
        asked = jnp.concatenate(asked, axis=0)
        scaled = (asked.astype(jnp.float32) * scales[0]).astype(jnp.bfloat16)
        score = lax.dot_general(
            scaled, keys, (((1,), (1,)), ((), ())), preferred_element_type=jnp.float32
        )
        score = jnp.where(place < limit, score, masked_fill)
        top = jnp.max(score, axis=1, keepdims=True)
        weight = jnp.exp2((score - top) * (inverse * log2e))
        top = top * inverse
        total = jnp.sum(weight, axis=1, keepdims=True)
        summed = jnp.dot(weight.astype(jnp.bfloat16), values, preferred_element_type=jnp.float32)
        for side in range(2):
            g = 2 * pair + side
            for block in range(8):
                source = slice(side * 64 + block * 8, side * 64 + block * 8 + 8)
                target = 2 * block + g // 4, slice((g % 4) * 8, (g % 4) * 8 + 8)
                part[target] = summed[source]
                tops[target], totals[target] = [
                    jnp.broadcast_to(value[source], (8, HD)) for value in (top, total)
                ]
    here = lax.broadcasted_iota(jnp.int32, (32, HD), 0) == lax.broadcasted_iota(
        jnp.int32, (32, HD), 1
    )
    for share in range(16):
        for at, column in enumerate((tops, totals)):
            part[share, 32 + at : 33 + at] = jnp.sum(
                jnp.where(here, column[share], 0.0), axis=0, keepdims=True
            )
    for copy in copies:
        copy.wait()


def attend(received, query, limits, own_scale, other_scale, page_table):
    rows = received[0].shape[0]
    pages = 2 * rows // PAGE
    heads = 512
    return pl.pallas_call(
        attend_kernel,
        in_specs=[SCALAR] + [WHOLE] * 8,
        out_specs=[ANYWHERE, WHOLE],
        scratch_shapes=[
            pltpu.VMEM((2, 2 * rows, HD), jnp.bfloat16),
            pltpu.VMEM((16, 32, HD), jnp.float32),
            pltpu.VMEM((16, 32, HD), jnp.float32),
            pltpu.SemaphoreType.DMA((2, pages)),
        ],
        out_shape=[
            jax.ShapeDtypeStruct((2, pages, PAGE, HD), jnp.bfloat16),
            jax.ShapeDtypeStruct((16, 40, HD), jnp.float32),
        ],
        compiler_params=params(VMEM),
        cost_estimate=cost(8 * heads * rows * HD, 16 * rows * HD, 2 * heads * rows),
    )(page_table, *in_vmem(received), query, limits, own_scale, other_scale)


def merge_kernel(parts, query, new_key, new_value, own_scale, other_scale, out, rows):
    yh, z, tp = [lax.axis_index(name) for name in ("yh", "z", "tp")]
    seen = pl.multiple_of(yh * 32, 32)
    step, at = z // 4, pl.multiple_of((z % 4) * 8, 8)
    half = 4 * HD
    rows[:, :half] = query[step, pl.ds(seen, 32), pl.ds(pl.multiple_of(tp * half, half), half)].astype(
        jnp.float32
    )
    rows[:, half : half + HD] = new_key[step, pl.ds(seen, 32)].astype(jnp.float32)
    rows[:, half + HD :] = new_value[step, pl.ds(seen, 32)].astype(jnp.float32)
    key = rows[pl.ds(at, 8), half : half + HD]
    value = rows[pl.ds(at, 8), half + HD :]
    scale = head_scale(own_scale, other_scale, 1)
    own = [
        jnp.sum(rows[pl.ds(at, 8), g * HD : (g + 1) * HD] * key, axis=1, keepdims=True) * inverse
        for g in range(4)
    ]
    own = jnp.concatenate(own, axis=0)
    value = jnp.concatenate([value] * 4, axis=0)
    here = lax.broadcasted_iota(jnp.int32, (1, 32, HD), 1) == lax.broadcasted_iota(
        jnp.int32, (1, 32, HD), 2
    )
    top, total = [
        jnp.sum(jnp.where(here, parts[:, at : at + 1, :], 0.0), axis=2, keepdims=True)
        for at in (32, 33)
    ]
    overall = jnp.maximum(jnp.max(top, axis=0), own)
    factor = jnp.exp(top - overall[None])
    own_weight = jnp.exp(own - overall)
    denominator = jnp.sum(total * factor, axis=0) + own_weight
    summed = jnp.sum(parts[:, :32, :] * factor, axis=0)
    result = (summed * scale + own_weight * value) / denominator
    out[...] = jnp.broadcast_to(result.astype(out.dtype)[None], out.shape)


def merge(parts, query, new_key, new_value, own_scale, other_scale):
    return pl.pallas_call(
        merge_kernel,
        in_specs=[WHOLE] * 6,
        out_specs=WHOLE,
        out_shape=jax.ShapeDtypeStruct((32, 32, HD), jnp.bfloat16),
        scratch_shapes=[pltpu.VMEM((32, 6 * HD), jnp.float32)],
        compiler_params=params(VMEM),
        cost_estimate=cost(1 << 18, 1 << 19, 512),
    )(*in_vmem([parts]), query, new_key, new_value, own_scale, other_scale)


def finish_kernel(whole, both, far, attended, scales):
    for yh in range(2):
        for step in range(2):
            for side in range(2):
                blocks = [
                    whole[yh * 16 + 2 * (step * 4 + part) + side].astype(jnp.float32)
                    for part in range(4)
                ]
                for g in range(4):
                    value = jnp.concatenate([b[g * 8 : g * 8 + 8] for b in blocks], axis=0)
                    head = side * 4 + g
                    attended[step, yh * 32 : yh * 32 + 32, head * HD : (head + 1) * HD] = (
                        value.astype(attended.dtype)
                    )
    tp, core = lax.axis_index("tp"), lax.axis_index("core")
    for side in range(2):
        for i in range(4):
            lanes = slice(i * HD, (i + 1) * HD)
            for c in range(2):
                own = jnp.where(core == c, both[0:1, lanes], far[0:1, lanes])
                other = jnp.where(core == c, both[1:2, lanes], far[1:2, lanes])
                scales[side : side + 1, (2 * i + c) * HD : (2 * i + c + 1) * HD] = jnp.where(
                    tp == side, own, other
                )


def finish(whole, both, far):
    return pl.pallas_call(
        finish_kernel,
        in_specs=[WHOLE] * 3,
        out_specs=[WHOLE] * 2,
        out_shape=[
            jax.ShapeDtypeStruct((2, 64, GROUP * HD), jnp.bfloat16),
            jax.ShapeDtypeStruct((2, 8 * HD), jnp.float32),
        ],
        compiler_params=params(VMEM),
        cost_estimate=cost(0, MIB // 2),
    )(*in_vmem([whole]), both, far)


def body(tokens, kv_weight, lengths, page_table, queries, new_keys, new_values, positions):
    sibling = send(tokens, core=1)
    own = keep(pltpu.with_memory_space_constraint(tokens, pltpu.HBM))

    def swapped(ids):
        return [(other, dz, False) for other, dz, _ in ids]

    at = lambda dz: [(0, dz, True), (1, dz - (1 if dz > 0 else -1), True)]
    near, far = lambda dz: [(0, dz, True)], lambda dz: [(1, dz, True)]
    part = lambda i: (i, 0, PIECE)

    first = take(kv_weight)
    cross, up, down = send(first, yh=1), send(first, z=1), send(first, z=-1)
    cross, up, down, both_up, both_down = relay(
        [cross, up, down], own, [[part(1), part(0)], [part(2), part(0)]]
    )
    wave = [(kv_weight, None), (both_up, at(-1)), (down, near(1))]

    over, under = send(both_up, x=-1), send(down, x=1)
    next_up, next_down = send(both_up, z=1), send(both_down, z=-1)
    sib = keep(sibling)
    up, down, last = relay([next_up, next_down], sib, [[part(0)]])
    wave += [(over, swapped(at(-1))), (under, swapped(near(1))), (up, at(-2)), (down, at(2))]
    (over,) = picked([over], [[part(0)]])

    side, over, under = send(over, yh=1), send(last, x=-1), send(down, x=1)
    next_up, next_down = send(up, z=1), send(down, z=-1)
    acc = project(own, sib, wave)[0]
    up, down, last, next_last = relay(
        [next_up, next_down], acc, [[part(0)], [(1, PIECE, PIECE)]]
    )
    wave = [(up, at(-3)), (down, at(3)), (over, swapped(near(-2))), (under, swapped(at(2)))]
    wave += [(side, swapped(far(-1)))]

    side, over, under = send(over, yh=1), send(last, x=-1), send(down, x=1)
    next_up, next_down = send(up, z=1), send(next_last, z=-1)
    acc = project(own, sib, wave, acc)[0]
    up, down, last, next_last = relay(
        [next_up, next_down], acc, [[part(0)], [(0, PIECE, PIECE)]]
    )
    wave = [(up, at(-4)), (down, far(3)), (over, swapped(near(-3))), (under, swapped(at(3)))]
    wave += [(side, swapped(far(-2)))]

    side, under, cross = send(over, yh=1), send(down, x=1), send(down, z=-1)
    corner, over = send(next_last, z=1, x=1), send(last, x=-1)
    acc = project(own, sib, wave, acc)[0]
    wave = [(over, swapped(near(-4))), (under, swapped(far(3))), (side, swapped(far(-3)))]
    wave += [(cross, far(-4)), (corner, swapped(far(-4)))]
    proj, squares = project(own, sib, wave, acc, lengths)
    squares = lax.all_to_all(squares, ("x", "z", "yh"), 0, 0, tiled=True)
    *sent, scale = quantize(proj, squares, lengths)

    received = []
    for k in range(4):
        pairs = []
        for t in range(2):
            for a in range(4):
                pairs.append((t * 4 + a, (a // 2) * 4 + (a + k + 2 * t) % 4))
        received.append(lax.ppermute(sent[k], ("tp", "x"), pairs))

    other_scale = send(scale, tp=1)
    both = jnp.concatenate([scale, other_scale], axis=0)
    far = send(both, core=1)

    kv_cache, part = attend(
        received, queries, positions.reshape(128, 1), scale, other_scale, page_table
    )
    parts = lax.all_to_all(part, ("z", "tp"), 0, 0, tiled=True)
    result = merge(parts, queries, new_keys, new_values, scale, other_scale)
    whole = lax.all_to_all(result, ("yh", "z", "tp"), 0, 0, tiled=True)
    attended, scales = finish(whole, both, far)
    return (kv_cache, scales, attended)


def solution(mesh):
    names = tuple(SIZES)
    fine = Mesh(mesh.devices.reshape(tuple(SIZES.values())), names)
    seq, head = ("yh", "z"), ("x", "core")
    in_specs = (
        P(seq + head, None),
        P(seq, "tp"),
        P(),
        P(seq + ("tp",)),
        P(None, None, head),
        P(None, None, head),
        P(None, None, head),
        P(),
    )
    out_specs = (P(None, seq + ("tp",), None, head), P(), P(None, None, head))
    return jax.shard_map(body, mesh=fine, in_specs=in_specs, out_specs=out_specs, check_vma=False)
```

```python
import functools
import math

import jax
import jax.numpy as jnp
from jax import lax
from jax.experimental import pallas as pl
from jax.experimental.pallas import tpu as pltpu
from jax.sharding import Mesh, PartitionSpec as P

HD = 128
PAGE = 256
PIECE = 256
TILE = 320
GROUP = 8
MIB = 1024 * 1024
VMEM = 20 * MIB
SHARED = 16 * MIB

eps = 1e-05
clip_level = 2.5
masked_fill = -1e30
inverse = 1.0 / (float(HD) ** 0.5)
log2e = 1.4426950408889634

SIZES = {"yh": 2, "z": 8, "tp": 2, "x": 4, "core": 2}
ANYWHERE = pl.BlockSpec(memory_space=pl.ANY)
WHOLE = pl.BlockSpec(memory_space=pltpu.VMEM)
SCALAR = pl.BlockSpec(memory_space=pltpu.SMEM)


def params(limit):
    return pltpu.CompilerParams(vmem_limit_bytes=limit)


def cost(flops=0, size=0, exps=0):
    return pl.CostEstimate(flops=flops, bytes_accessed=size, transcendentals=exps)


def send(value, **steps):
    names = tuple(steps)
    sizes = [SIZES[name] for name in names]
    pairs = []
    for i in range(math.prod(sizes)):
        target, rest = 0, i
        place = []
        for n in reversed(sizes):
            place.insert(0, rest % n)
            rest //= n
        for at, n, name in zip(place, sizes, names):
            target = target * n + (at + steps[name]) % n
        pairs.append((i, target))
    return lax.ppermute(value, names if len(names) > 1 else names[0], pairs)


def in_vmem(values):
    return [pltpu.with_memory_space_constraint(value, pltpu.VMEM) for value in values]


def relay_kernel(count, picks, *refs):
    sources, outs, sems = refs[:count], refs[count + 1 + count : -1], refs[-1]
    copies = []
    for out, parts in zip(outs, picks):
        at = 0
        for i, start, rows in parts:
            copies.append(
                pltpu.make_async_copy(
                    sources[i].at[pl.ds(start, rows)], out.at[pl.ds(at, rows)], sems.at[len(copies)]
                )
            )
            at += rows
    for copy in copies:
        copy.start()
    for copy in copies:
        copy.wait()


def relay(values, after, picks=()):
    args = in_vmem(values)
    shapes = [jax.ShapeDtypeStruct(v.shape, v.dtype) for v in values]
    for parts in picks:
        shape = (sum(rows for _, _, rows in parts), values[0].shape[1])
        shapes.append(pltpu.VMEM(shape, values[0].dtype))
    return pl.pallas_call(
        functools.partial(relay_kernel, len(args), picks),
        in_specs=[ANYWHERE] * (len(args) + 1),
        out_specs=[ANYWHERE] * len(shapes),
        out_shape=shapes,
        input_output_aliases={i: i for i in range(len(args))},
        scratch_shapes=[
            pltpu.SemaphoreType.DMA((max(1, sum(len(p) for p in picks)),)),
        ],
        compiler_params=params(SHARED),
        cost_estimate=cost(),
    )(*args, after)


def picked_kernel(count, picks, *refs):
    relay_kernel(count, picks, *refs[:count], None, *[None] * count, *refs[count:])


def picked(values, picks):
    return pl.pallas_call(
        functools.partial(picked_kernel, len(values), picks),
        in_specs=[ANYWHERE] * len(values),
        out_specs=[ANYWHERE] * len(picks),
        out_shape=[
            pltpu.VMEM((sum(rows for _, _, rows in parts), values[0].shape[1]), values[0].dtype)
            for parts in picks
        ],
        scratch_shapes=[pltpu.SemaphoreType.DMA((sum(len(p) for p in picks),))],
        compiler_params=params(SHARED),
        cost_estimate=cost(),
    )(*in_vmem(values))


def keep_kernel(source, target, sem):
    copy = pltpu.make_async_copy(source, target, sem)
    copy.start()
    copy.wait()


def keep(value):
    return pl.pallas_call(
        keep_kernel,
        in_specs=[ANYWHERE],
        out_specs=ANYWHERE,
        out_shape=pltpu.VMEM(value.shape, value.dtype),
        scratch_shapes=[pltpu.SemaphoreType.DMA],
        compiler_params=params(SHARED),
        cost_estimate=cost(size=2 * value.size * value.dtype.itemsize),
    )(value)


def take_kernel(weight, out, sems):
    core, half = lax.axis_index("core"), lax.axis_index("x") % 2
    copies = []
    for i in range(4):
        copies.append(
            pltpu.make_async_copy(
                weight.at[
                    pl.ds(pl.multiple_of(half * PIECE, PIECE), PIECE),
                    pl.ds(pl.multiple_of((2 * i + core) * HD, HD), HD),
                ],
                out.at[:, pl.ds(i * HD, HD)],
                sems.at[i],
            )
        )
    for copy in copies:
        copy.start()
    for copy in copies:
        copy.wait()


def take(weight):
    return pl.pallas_call(
        take_kernel,
        in_specs=[ANYWHERE],
        out_specs=ANYWHERE,
        out_shape=pltpu.VMEM((PIECE, 4 * HD), weight.dtype),
        scratch_shapes=[pltpu.SemaphoreType.DMA((4,))],
        compiler_params=params(SHARED),
        cost_estimate=cost(size=MIB),
    )(weight)


def project_kernel(names, has_acc, last, own, sib, *refs):
    arrays = len(names)
    sources, refs = refs[:arrays], refs[arrays:]
    acc = lengths = None
    if has_acc:
        acc, refs = refs[0], refs[1:]
    if last:
        lengths, refs = refs[0], refs[1:]
    outs, (held, sems) = refs[:-2], refs[-2:]
    yh, z, x = lax.axis_index("yh"), lax.axis_index("z"), lax.axis_index("x")
    core = lax.axis_index("core")
    width = 4 * HD
    copies, columns, weights = [], [], []
    for source, pieces in zip(sources, names):
        if pieces is None:
            pieces = [(0, 0, None), (0, 0, None)]
            for j in range(4):
                lanes = pl.ds(pl.multiple_of((2 * j + core) * HD, HD), HD)
                copies.append(
                    pltpu.make_async_copy(
                        source.at[:, lanes], held.at[:, pl.ds(j * HD, HD)], sems.at[j]
                    )
                )
            source = held
        for j, (other, dz, mine) in enumerate(pieces):
            half = j if mine is None else (x + (0 if mine else 1)) % 2
            shard = ((yh + other) % 2) * 8 + (z + dz + 8) % 8
            columns.append(pl.multiple_of((shard * 2 + half) * PIECE, PIECE))
            weights.append((source, j * PIECE))
    for copy in copies:
        copy.start()
    for copy in copies:
        copy.wait()
    rows = own.shape[0]
    total = refs[-3] if last else outs[0]
    for piece, (column, (source, start)) in enumerate(zip(columns, weights)):
        weight = source[start : start + PIECE]
        for side, tokens in enumerate((own, sib)):
            for row in range(0, rows, TILE):
                value = jnp.dot(
                    tokens[pl.ds(row, TILE), pl.ds(column, PIECE)],
                    weight,
                    preferred_element_type=jnp.float32,
                )
                here = pl.ds(side * rows + row, TILE)
                if piece > 0:
                    total[here] += value
                elif has_acc:
                    total[here] = acc[here] + value
                else:
                    total[here] = value
    if not last:
        return
    squares = outs[1]
    part = jnp.zeros((1, width), jnp.float32)
    limit = jnp.where(yh == 0, lengths[0], lengths[1])
    for row in range(0, 2 * rows, TILE):
        value = total[row : row + TILE]
        goes = pl.multiple_of((row + core * rows) % (2 * rows), TILE)
        place = (z * 4 + x) * 2 * rows + goes + lax.broadcasted_iota(jnp.int32, value.shape, 0)
        kept = jnp.where(place < limit, value * value, 0.0)
        part = part + jnp.sum(kept, axis=0, keepdims=True)
        outs[0][pl.ds(goes, TILE)] = value
    for i in range(4):
        lanes = part[None, :, i * HD : (i + 1) * HD]
        squares[:, i : i + 1, :] = jnp.broadcast_to(lanes, (squares.shape[0], 1, HD))


def project(own, sib, pieces, acc=None, lengths=None):
    names = [ids for _, ids in pieces]
    n = sum(2 if ids is None else len(ids) for ids in names)
    rows, width = own.shape[0], 4 * HD
    last = lengths is not None
    in_specs = [WHOLE, WHOLE] + [ANYWHERE if ids is None else WHOLE for ids in names]
    args = [own, sib] + [value for value, _ in pieces]
    args = [
        value if spec is ANYWHERE else pltpu.with_memory_space_constraint(value, pltpu.VMEM)
        for value, spec in zip(args, in_specs)
    ]
    aliases = {}
    if acc is not None:
        in_specs.append(WHOLE)
        if not last:
            aliases = {len(args): 0}
        args.append(acc)
    scratch = [
        pltpu.VMEM((2 * PIECE, width), jnp.bfloat16),
        pltpu.SemaphoreType.DMA((4,)),
    ]
    if not last:
        out_shape = [pltpu.VMEM((2 * rows, width), jnp.float32)]
    else:
        in_specs.append(SCALAR)
        args.append(lengths)
        out_shape = [pltpu.VMEM((2 * rows, width), jnp.float32)]
        out_shape.append(jax.ShapeDtypeStruct((64, 4, HD), jnp.float32))
        scratch.insert(0, pltpu.VMEM((2 * rows, width), jnp.float32))
    return pl.pallas_call(
        functools.partial(project_kernel, names, acc is not None, last),
        in_specs=in_specs,
        out_specs=[WHOLE] * len(out_shape),
        scratch_shapes=scratch,
        out_shape=out_shape,
        input_output_aliases=aliases,
        compiler_params=params(SHARED),
        cost_estimate=cost(4 * rows * PIECE * n * width, n * PIECE * width * 2),
    )(*args)


def quantize_kernel(proj, squares, lengths, *outs):
    x, tp = lax.axis_index("x"), lax.axis_index("tp")
    count = (lengths[0] + lengths[1]).astype(jnp.float32)
    mean = jnp.sum(squares[...], axis=0) / count
    for i in range(4):
        outs[4][:, i * HD : (i + 1) * HD] = jnp.sqrt(mean[i : i + 1] + eps)
    for k in range(4):
        head = pl.ds(pl.multiple_of(((x + k + 2 * tp) % 4) * HD, HD), HD)
        value = proj[:, head] * (1.0 / outs[4][:, head])
        outs[k][...] = jnp.clip(value, -clip_level, clip_level).astype(jnp.bfloat16)


def quantize(proj, squares, lengths):
    rows, width = proj.shape
    return pl.pallas_call(
        quantize_kernel,
        in_specs=[WHOLE, WHOLE, SCALAR],
        out_specs=[WHOLE] * 5,
        out_shape=[pltpu.VMEM((rows, HD), jnp.bfloat16)] * 4
        + [jax.ShapeDtypeStruct((1, width), jnp.float32)],
        compiler_params=params(VMEM),
        cost_estimate=cost(4 * rows * width, 6 * rows * width),
    )(pltpu.with_memory_space_constraint(proj, pltpu.VMEM), squares, lengths)


def head_scale(own, other, side):
    here = pl.ds(pl.multiple_of(lax.axis_index("x") * HD, HD), HD)
    return jnp.where(lax.axis_index("tp") == side, own[:, here], other[:, here])


def attend_kernel(
    pages, r0, r1, r2, r3, query, limits, own_scale, other_scale, cache, part, held, sums, tops, totals, sems
):
    yh, z, x, tp = [lax.axis_index(name) for name in ("yh", "z", "x", "tp")]
    got = (r0, r1, r2, r3)
    rows = r0.shape[0]
    scales = [head_scale(own_scale, other_scale, side) for side in range(2)]
    first = (x - 2 * tp + 4) % 4
    for m in range(4):

        @pl.when(first == m)
        def _(m=m):
            for j in range(4):
                held[j // 2, pl.ds((j % 2) * rows, rows)] = got[(m - j) % 4][...]

    count = 2 * rows // PAGE
    copies = []
    for j in range(2):
        for b in range(count):
            copies.append(
                pltpu.make_async_copy(
                    held.at[j, pl.ds(b * PAGE, PAGE)], cache.at[j, pages[b]], sems.at[j, b]
                )
            )
    for copy in copies:
        copy.start()
    keys, values = held[0], held[1]
    seen = pl.multiple_of(yh * 32, 32)
    limit = jnp.concatenate([limits[pl.ds(s * 64 + seen, 32)] for s in range(2)], axis=0)
    limit = jnp.concatenate([limit, limit], axis=0)
    place = (z * 2 + tp) * 2 * rows + lax.broadcasted_iota(jnp.int32, (1, 2 * rows), 1)
    for pair in range(GROUP // 2):
        asked = [
            query[s, pl.ds(seen, 32), g * HD : (g + 1) * HD]
            for g in (2 * pair, 2 * pair + 1)
            for s in range(2)
        ]
        asked = jnp.concatenate(asked, axis=0)
        scaled = (asked.astype(jnp.float32) * scales[0]).astype(jnp.bfloat16)
        score = lax.dot_general(
            scaled, keys, (((1,), (1,)), ((), ())), preferred_element_type=jnp.float32
        )
        score = jnp.where(place < limit, score, masked_fill)
        top = jnp.max(score, axis=1, keepdims=True)
        weight = jnp.exp2((score - top) * (inverse * log2e))
        top = top * inverse
        total = jnp.sum(weight, axis=1, keepdims=True)
        summed = jnp.dot(weight.astype(jnp.bfloat16), values, preferred_element_type=jnp.float32)
        for side in range(2):
            g = 2 * pair + side
            for block in range(8):
                source = slice(side * 64 + block * 8, side * 64 + block * 8 + 8)
                target = 2 * block + g // 4, slice((g % 4) * 8, (g % 4) * 8 + 8)
                sums[target] = summed[source]
                tops[target], totals[target] = [
                    jnp.broadcast_to(value[source], (8, HD)) for value in (top, total)
                ]
    here = lax.broadcasted_iota(jnp.int32, (32, HD), 0) == lax.broadcasted_iota(
        jnp.int32, (32, HD), 1
    )
    for share in range(16):
        part[share, 0:32] = sums[share].astype(part.dtype)
        lines = []
        for column in (tops, totals):
            line = jnp.sum(jnp.where(here, column[share], 0.0), axis=0, keepdims=True)
            for _ in range(3):
                piece = line.astype(jnp.bfloat16).astype(jnp.float32)
                lines.append(piece)
                line = line - piece
        lines.append(jnp.zeros((10, HD), jnp.float32))
        part[share, 32:48] = jnp.concatenate(lines, axis=0).astype(part.dtype)
    for copy in copies:
        copy.wait()


def attend(received, query, limits, own_scale, other_scale, page_table):
    rows = received[0].shape[0]
    pages = 2 * rows // PAGE
    heads = 512
    return pl.pallas_call(
        attend_kernel,
        in_specs=[SCALAR] + [WHOLE] * 8,
        out_specs=[ANYWHERE, WHOLE],
        scratch_shapes=[
            pltpu.VMEM((2, 2 * rows, HD), jnp.bfloat16),
            pltpu.VMEM((16, 32, HD), jnp.float32),
            pltpu.VMEM((16, 32, HD), jnp.float32),
            pltpu.VMEM((16, 32, HD), jnp.float32),
            pltpu.SemaphoreType.DMA((2, pages)),
        ],
        out_shape=[
            jax.ShapeDtypeStruct((2, pages, PAGE, HD), jnp.bfloat16),
            jax.ShapeDtypeStruct((16, 48, HD), jnp.bfloat16),
        ],
        compiler_params=params(VMEM),
        cost_estimate=cost(8 * heads * rows * HD, 16 * rows * HD, 2 * heads * rows),
    )(page_table, *in_vmem(received), query, limits, own_scale, other_scale)


def merge_kernel(parts, query, new_key, new_value, own_scale, other_scale, out, rows):
    yh, z, tp = [lax.axis_index(name) for name in ("yh", "z", "tp")]
    seen = pl.multiple_of(yh * 32, 32)
    step, at = z // 4, pl.multiple_of((z % 4) * 8, 8)
    half = 4 * HD
    rows[:, :half] = query[step, pl.ds(seen, 32), pl.ds(pl.multiple_of(tp * half, half), half)].astype(
        jnp.float32
    )
    rows[:, half : half + HD] = new_key[step, pl.ds(seen, 32)].astype(jnp.float32)
    rows[:, half + HD :] = new_value[step, pl.ds(seen, 32)].astype(jnp.float32)
    key = rows[pl.ds(at, 8), half : half + HD]
    value = rows[pl.ds(at, 8), half + HD :]
    scale = head_scale(own_scale, other_scale, 1)
    own = [
        jnp.sum(rows[pl.ds(at, 8), g * HD : (g + 1) * HD] * key, axis=1, keepdims=True) * inverse
        for g in range(4)
    ]
    own = jnp.concatenate(own, axis=0)
    value = jnp.concatenate([value] * 4, axis=0)
    here = lax.broadcasted_iota(jnp.int32, (1, 32, HD), 1) == lax.broadcasted_iota(
        jnp.int32, (1, 32, HD), 2
    )
    lines = parts[:, 32:48, :].astype(jnp.float32)
    top, total = [
        jnp.sum(
            jnp.where(here, lines[:, at : at + 1] + lines[:, at + 1 : at + 2] + lines[:, at + 2 : at + 3], 0.0),
            axis=2,
            keepdims=True,
        )
        for at in (0, 3)
    ]
    overall = jnp.maximum(jnp.max(top, axis=0), own)
    factor = jnp.exp(top - overall[None])
    own_weight = jnp.exp(own - overall)
    denominator = jnp.sum(total * factor, axis=0) + own_weight
    summed = jnp.sum(parts[:, :32, :].astype(jnp.float32) * factor, axis=0)
    result = (summed * scale + own_weight * value) / denominator
    out[...] = jnp.broadcast_to(result.astype(out.dtype)[None], out.shape)


def merge(parts, query, new_key, new_value, own_scale, other_scale):
    return pl.pallas_call(
        merge_kernel,
        in_specs=[WHOLE] * 6,
        out_specs=WHOLE,
        out_shape=jax.ShapeDtypeStruct((32, 32, HD), jnp.bfloat16),
        scratch_shapes=[pltpu.VMEM((32, 6 * HD), jnp.float32)],
        compiler_params=params(VMEM),
        cost_estimate=cost(1 << 18, 1 << 19, 512),
    )(*in_vmem([parts]), query, new_key, new_value, own_scale, other_scale)


def finish_kernel(whole, both, far, attended, scales):
    for yh in range(2):
        for step in range(2):
            for side in range(2):
                blocks = [
                    whole[yh * 16 + 2 * (step * 4 + part) + side].astype(jnp.float32)
                    for part in range(4)
                ]
                for g in range(4):
                    value = jnp.concatenate([b[g * 8 : g * 8 + 8] for b in blocks], axis=0)
                    head = side * 4 + g
                    attended[step, yh * 32 : yh * 32 + 32, head * HD : (head + 1) * HD] = (
                        value.astype(attended.dtype)
                    )
    tp, core = lax.axis_index("tp"), lax.axis_index("core")
    for side in range(2):
        for i in range(4):
            lanes = slice(i * HD, (i + 1) * HD)
            for c in range(2):
                own = jnp.where(core == c, both[0:1, lanes], far[0:1, lanes])
                other = jnp.where(core == c, both[1:2, lanes], far[1:2, lanes])
                scales[side : side + 1, (2 * i + c) * HD : (2 * i + c + 1) * HD] = jnp.where(
                    tp == side, own, other
                )


def finish(whole, both, far):
    return pl.pallas_call(
        finish_kernel,
        in_specs=[WHOLE] * 3,
        out_specs=[WHOLE] * 2,
        out_shape=[
            jax.ShapeDtypeStruct((2, 64, GROUP * HD), jnp.bfloat16),
            jax.ShapeDtypeStruct((2, 8 * HD), jnp.float32),
        ],
        compiler_params=params(VMEM),
        cost_estimate=cost(0, MIB // 2),
    )(*in_vmem([whole]), both, far)


def body(tokens, kv_weight, lengths, page_table, queries, new_keys, new_values, positions):
    sibling = send(tokens, core=1)
    own = keep(pltpu.with_memory_space_constraint(tokens, pltpu.HBM))

    def swapped(ids):
        return [(other, dz, False) for other, dz, _ in ids]

    at = lambda dz: [(0, dz, True), (1, dz - (1 if dz > 0 else -1), True)]
    near, far = lambda dz: [(0, dz, True)], lambda dz: [(1, dz, True)]
    part = lambda i: (i, 0, PIECE)

    first = take(kv_weight)
    cross, up, down = send(first, yh=1), send(first, z=1), send(first, z=-1)
    cross, up, down, both_up, both_down = relay(
        [cross, up, down], own, [[part(1), part(0)], [part(2), part(0)]]
    )
    wave = [(kv_weight, None), (both_up, at(-1)), (down, near(1))]

    over, under = send(both_up, x=-1), send(down, x=1)
    next_up, next_down = send(both_up, z=1), send(both_down, z=-1)
    sib = keep(sibling)
    up, down, last = relay([next_up, next_down], sib, [[part(0)]])
    wave += [(over, swapped(at(-1))), (under, swapped(near(1))), (up, at(-2)), (down, at(2))]
    (over,) = picked([over], [[part(0)]])

    side, over, under = send(over, yh=1), send(last, x=-1), send(down, x=1)
    next_up, next_down = send(up, z=1), send(down, z=-1)
    acc = project(own, sib, wave)[0]
    up, down, last, next_last = relay(
        [next_up, next_down], acc, [[part(0)], [(1, PIECE, PIECE)]]
    )
    wave = [(up, at(-3)), (down, at(3)), (over, swapped(near(-2))), (under, swapped(at(2)))]
    wave += [(side, swapped(far(-1)))]

    side, over, under = send(over, yh=1), send(last, x=-1), send(down, x=1)
    next_up, next_down = send(up, z=1), send(next_last, z=-1)
    acc = project(own, sib, wave, acc)[0]
    up, down, last, next_last = relay(
        [next_up, next_down], acc, [[part(0)], [(0, PIECE, PIECE)]]
    )
    wave = [(up, at(-4)), (down, far(3)), (over, swapped(near(-3))), (under, swapped(at(3)))]
    wave += [(side, swapped(far(-2)))]

    side, under, cross = send(over, yh=1), send(down, x=1), send(down, z=-1)
    corner, over = send(next_last, z=1, x=1), send(last, x=-1)
    acc = project(own, sib, wave, acc)[0]
    wave = [(over, swapped(near(-4))), (under, swapped(far(3))), (side, swapped(far(-3)))]
    wave += [(cross, far(-4)), (corner, swapped(far(-4)))]
    proj, squares = project(own, sib, wave, acc, lengths)
    squares = lax.all_to_all(squares, ("x", "z", "yh"), 0, 0, tiled=True)
    *sent, scale = quantize(proj, squares, lengths)

    received = []
    for k in range(4):
        pairs = []
        for t in range(2):
            for a in range(4):
                pairs.append((t * 4 + a, (a // 2) * 4 + (a + k + 2 * t) % 4))
        received.append(lax.ppermute(sent[k], ("tp", "x"), pairs))

    other_scale = send(scale, tp=1)
    both = jnp.concatenate([scale, other_scale], axis=0)
    far = send(both, core=1)

    kv_cache, part = attend(
        received, queries, positions.reshape(128, 1), scale, other_scale, page_table
    )
    parts = lax.all_to_all(part, ("z", "tp"), 0, 0, tiled=True)
    result = merge(parts, queries, new_keys, new_values, scale, other_scale)
    whole = lax.all_to_all(result, ("yh", "z", "tp"), 0, 0, tiled=True)
    attended, scales = finish(whole, both, far)
    return (kv_cache, scales, attended)


def solution(mesh):
    names = tuple(SIZES)
    fine = Mesh(mesh.devices.reshape(tuple(SIZES.values())), names)
    seq, head = ("yh", "z"), ("x", "core")
    in_specs = (
        P(seq + head, None),
        P(seq, "tp"),
        P(),
        P(seq + ("tp",)),
        P(None, None, head),
        P(None, None, head),
        P(None, None, head),
        P(),
    )
    out_specs = (P(None, seq + ("tp",), None, head), P(), P(None, None, head))
    return jax.shard_map(body, mesh=fine, in_specs=in_specs, out_specs=out_specs, check_vma=False)
```
